256 devices in a mesh: ctx: 32 (over y_hi, z, core), ch: 8 (over y_lo, x).
Axes of the slice: x: 4, y: 4 (y_hi: 2, y_lo: 2; y = y_hi * 2 + y_lo), z: 8, core: 2. Of those that a mesh axis runs over, the one named last changes fastest.
Arguments:
- projected: bfloat16 [3, 8192, 4096], P(None, 'ctx', 'ch'), may hold values from -6 to 6
- short_filter: float32 [3, 7, 4096], P(None, None, 'ch'), may hold values from -3 to 3
- residues: float32 [16, 4096], P(None, 'ch'), may hold values from -0.6 to 0.6
- decay_rates: float32 [16, 4096], P(None, 'ch'), may hold values from 0.0001 to 0.05
- doc_blocks: int32 [16], replicated, may hold values from 1 to 32, 64 in all
- out_weight: bfloat16 [4096, 4096], P('ctx', 'ch'), may hold values from -0.09375 to 0.09375
Outputs:
- mixed: bfloat16 [8192, 4096], P('ctx', 'ch')
The draws below stay inside these ranges and needn't reach their ends.
Inputs may be any that keep to these rules, and one draw needn't show every extreme that they name: `doc_blocks`: each length counts blocks of 128 tokens; the lengths sum to 8192 // 128, and one sequence has exactly 32 blocks.
All inputs are finite; a program needn't handle non-finite values.
Results may differ from the reference program's by a relative error of at most 0.0049.
Values may be sent and summed in bfloat16 or wider, within the bound.
A program may use at most 64 MiB of HBM per device.

```python
import math
import jax
import jax.numpy as jnp
import numpy as np
from jax import lax

D = 4096
ORDER = 16
SHORT = 7
BLK = 128
NDOCS = 16
TOKENS = 8192
DOC_MOST = 32


def shard_levels(rng, extent, pieces, low, top_value):
    level, own = 1.0, jax.random.fold_in(rng, 6)
    for position, shards_of in pieces:
        draws = jnp.exp(jax.random.uniform(jax.random.fold_in(own, position), (shards_of,), jnp.float32, low / len(pieces), top_value / len(pieces)))
        level = level * jnp.repeat(draws, extent[position] // shards_of).reshape([-1 if axis == position else 1 for axis in range(len(extent))])
    return level


def profile(amount, total, limit, skew):
    loads = [(1 << 20) // math.isqrt(grade ** skew) + 1 for grade in range(2, amount + 1)]
    spare, counts = total - limit - (amount - 1), [1] * (amount - 1)
    while spare > 0:
        candidates = [i for i in range(amount - 1) if counts[i] < limit]
        pool, left = sum([loads[i] for i in candidates]), spare
        for i in candidates:
            addition = min(limit - counts[i], max(1, left * loads[i] // pool), spare)
            counts[i] = counts[i] + addition
            spare = spare - addition
    return np.array([limit] + counts)


def uneven(stream_key, count, total, most, skew):
    if count == 2:
        one = jax.random.randint(stream_key, (), max(1, total - most), min(most, total - 1) + 1)
        return jnp.stack([one, total - one])
    sizes = jnp.asarray(profile(count, total, most, skew), jnp.int32)
    couples = (count - 1) // 2
    giver, taker = sizes[1:1 + 2 * couples:2], sizes[2:2 + 2 * couples:2]
    slack = jnp.minimum(giver - 1, most - taker)
    passed = jax.random.randint(jax.random.fold_in(stream_key, 1), (couples,), 0, 1 << 20) % (slack + 1)
    sizes = sizes.at[1:1 + 2 * couples:2].set(giver - passed).at[2:2 + 2 * couples:2].set(taker + passed)
    return sizes[jax.random.permutation(jax.random.fold_in(stream_key, 2), count)]


def noise(rng, extent, width, most, split=(), kind=jnp.bfloat16):
    values = jax.random.normal(rng, extent, jnp.float32) * width
    if len(split) > 0:
        values = shard_levels(rng, extent, split, -0.22, 0.18) * values
    return jnp.clip(values, min=-most, max=most).astype(kind)


def setup_inputs(seed: int = 0) -> dict:
    keys = jax.random.split(jax.random.key(seed), 7)
    return {
        "projected": noise(keys[0], (3, TOKENS, D), 1.0, 6.0, ((1, 32), (2, 8))),
        "short_filter": noise(keys[1], (3, SHORT, D), 0.5, 3.0, ((2, 8),), jnp.float32),
        "residues": noise(keys[2], (ORDER, D), 0.1, 0.6, ((1, 8),), jnp.float32),
        "decay_rates": jnp.clip(jnp.exp(math.log(0.05) - 6.214608 * jax.random.uniform(keys[3], (ORDER, D), jnp.float32) ** shard_levels(keys[3], (ORDER, D), ((1, 8),), -0.2, 0.2)), 0.0001, 0.05),
        "doc_blocks": uneven(keys[4], NDOCS, TOKENS // BLK, DOC_MOST, 2).astype(jnp.int32),
        "out_weight": noise(keys[5], (D, D), D ** -0.5, 0.09375, ((0, 32), (1, 8))),
    }


def reference(projected, short_filter, residues, decay_rates, doc_blocks, out_weight):
    nblk = TOKENS // BLK
    ends = jnp.cumsum(doc_blocks)
    starts_at = ends - doc_blocks
    block_ids = jnp.arange(nblk, dtype=jnp.int32)
    is_start = jnp.any(block_ids[:, None] == starts_at[None, :], axis=1)
    start_tok = jnp.repeat(is_start, BLK, total_repeat_length=TOKENS)
    within = jnp.arange(TOKENS, dtype=jnp.int32) % BLK
    convs = []
    for stream in range(3):
        inputs = projected[stream].astype(jnp.float32)
        total = jnp.zeros((TOKENS, D), jnp.float32)
        for tap in range(SHORT):
            keep = jnp.logical_or(within >= tap, jnp.logical_not(start_tok)).astype(jnp.float32)
            shifted = jnp.pad(inputs, ((tap, 0), (0, 0)))[:TOKENS]
            total = total + short_filter[stream, tap][None, :] * shifted * keep[:, None]
        convs.append(total)
    query, keyed, valued = convs
    blocked = (keyed * valued).reshape(nblk, BLK, D)
    lags = jnp.arange(BLK, dtype=jnp.float32)
    head = jnp.sum(residues[:, None, :] * jnp.exp(-decay_rates[:, None, :] * lags[None, :, None]), axis=0)
    span = 2 * BLK
    head_spec = jnp.fft.rfft(head, n=span, axis=0)

    def intra_group(group):
        spec = jnp.fft.rfft(group, n=span, axis=1) * head_spec[None]
        return jnp.fft.irfft(spec, n=span, axis=1)[:, :BLK].astype(jnp.float32)

    intra = lax.map(intra_group, blocked.reshape(nblk // 4, 4, BLK, D)).reshape(nblk, BLK, D)
    tail = jnp.exp(-decay_rates[:, None, :] * (BLK - 1 - lags)[None, :, None])
    own_end = jnp.einsum("rsc,jsc->jrc", tail, blocked, precision=lax.Precision.HIGHEST)
    step_decay = jnp.exp(-decay_rates * BLK)

    def advance(carry, inputs):
        own, begin = inputs
        entering = jnp.where(begin, jnp.zeros_like(carry), carry)
        return step_decay * entering + own, entering

    _, states = lax.scan(advance, jnp.zeros((ORDER, D), jnp.float32), (own_end, is_start))
    reach = residues[:, None, :] * jnp.exp(-decay_rates[:, None, :] * (lags + 1.0)[None, :, None])
    inter = jnp.einsum("rtc,jrc->jtc", reach, states, precision=lax.Precision.HIGHEST)
    response = (intra + inter).reshape(TOKENS, D)
    hidden = (query * response).astype(jnp.bfloat16)
    return jnp.dot(hidden, out_weight, preferred_element_type=jnp.float32).astype(jnp.bfloat16)
```

```python
import functools

import jax
import jax.numpy as jnp
import ml_dtypes
import numpy as np
from jax import lax
from jax.experimental import pallas as pl
from jax.experimental.pallas import tpu as pltpu
from jax.sharding import PartitionSpec as P

ORDER = 16
SHORT = 7
BLK = 128
LANES = 128
MESH = pl.DeviceIdType.MESH
F32, BF16 = jnp.float32, jnp.bfloat16


def dft_tables():
    freq = np.arange(BLK)[:, None] + 0.5
    angles = 2.0 * np.pi * freq * np.arange(BLK)[None, :] / (2 * BLK)
    table = np.concatenate([np.cos(angles), np.sin(angles)], axis=0)

    def split(a):
        high = a.astype(ml_dtypes.bfloat16)
        low = (a - high.astype(np.float64)).astype(ml_dtypes.bfloat16)
        return np.concatenate([high, high, low], axis=1)

    return split(table), split(table.T)


def split_rows(a):
    high = a.astype(BF16)
    low = (a - high.astype(F32)).astype(BF16)
    return jnp.concatenate([high, low, high], axis=0)


def kernel(
    proj, sf, res, dec, docs, w, fwd, inv, out,
    halo, ext, query, source, spec, intra, head, hspec,
    parts, rx, back, rx2, dparts, through, state, ends_own,
    wbuf, hbuf, acc,
    halo_sem, a2a_sem, ws, wr, hs, hr,
):
    p, q = lax.axis_index("ctx"), lax.axis_index("ch")
    n_ctx = lax.axis_size("ctx")
    core = p % 2
    z = (p // 2) % 8
    y_hi = p // 16
    x, y_lo = q % 4, q // 4

    def ctx_of(hi, zz, cc):
        return hi * 16 + zz * 2 + cc

    q_right = y_lo * 4 + (x + 1) % 4
    q_left = y_lo * 4 + (x + 3) % 4
    q_opp = y_lo * 4 + (x + 2) % 4
    q_y = (1 - y_lo) * 4 + x
    q_yright = (1 - y_lo) * 4 + (x + 1) % 4
    q_yleft = (1 - y_lo) * 4 + (x + 3) % 4
    q_yopp = (1 - y_lo) * 4 + (x + 2) % 4

    def remote(src, dst, send, recv, to_ctx, to_ch):
        return pltpu.make_async_remote_copy(
            src_ref=src, dst_ref=dst, send_sem=send, recv_sem=recv,
            device_id=(to_ctx, to_ch), device_id_type=MESH,
        )

    barrier = pltpu.get_barrier_semaphore()

    def greet(o, carry):
        pl.semaphore_signal(barrier, inc=1, device_id=((p + o) % n_ctx, q), device_id_type=MESH)
        return carry

    lax.fori_loop(1, n_ctx, greet, 0)
    for to in (q_right, q_left, q_y):
        pl.semaphore_signal(barrier, inc=1, device_id=(p, to), device_id_type=MESH)
    pl.semaphore_wait(barrier, n_ctx - 1 + 3)

    halo_copy = remote(
        proj.at[:, pl.ds(240, 16), :], halo, halo_sem.at[0], halo_sem.at[1], (p + 1) % n_ctx, q
    )
    halo_copy.start()

    step = 1 - 2 * core
    z_next = (z + step + 8) % 8
    hi_of = (y_hi, 1 - y_hi)
    sends = []

    def started(copy):
        copy.start()
        sends.append(copy)

    def half(hi, zz, cc):
        return wbuf.at[hi, zz, pl.ds(cc * 128, 128), :]

    def spread(plane, src):
        hi = hi_of[plane]
        dst = half(hi, z, core)
        started(remote(src, dst, ws.at[plane, 1], wr.at[plane, 1 + core], ctx_of(y_hi, (z + 1) % 8, 0), q))
        started(remote(src, dst, ws.at[plane, 2], wr.at[plane, 1 + core], ctx_of(y_hi, (z + 7) % 8, 1), q))
        started(remote(src, dst, ws.at[plane, 6], wr.at[plane, 6], ctx_of(y_hi, z, 1 - core), q))

    def landed(ref, sem):
        pltpu.make_async_copy(ref, ref, sem).wait()

    def pass_on(plane, hop):
        hi = hi_of[plane]
        oz = (z - step * hop + 8) % 8
        whole = wbuf.at[hi, oz]
        mine = half(hi, oz, core)
        if hop == 1:
            landed(half(hi, oz, 0), wr.at[plane, 1])
            landed(half(hi, oz, 1), wr.at[plane, 2])
        elif hop < 4:
            landed(whole, wr.at[plane, 1 + hop])
        else:
            landed(mine, wr.at[plane, 5])
        if hop < 3:
            started(remote(whole, whole, ws.at[plane, 2 + hop], wr.at[plane, 2 + hop], ctx_of(y_hi, z_next, core), q))
        elif hop == 3:
            started(remote(mine, mine, ws.at[plane, 5], wr.at[plane, 5], ctx_of(y_hi, z_next, core), q))
        part = whole if hop < 4 else mine
        started(remote(part, part, ws.at[plane, 6 + hop], wr.at[plane, 6 + hop], ctx_of(y_hi, z, 1 - core), q))

    spread(0, w)
    started(
        remote(w, half(y_hi, z, core), ws.at[1, 0], wr.at[1, 0], ctx_of(1 - y_hi, z, core), q)
    )
    half(y_hi, z, core)[...] = w[...]

    begins0, begins1, at = jnp.float32(0), jnp.float32(0), jnp.int32(0)
    rows = lax.broadcasted_iota(jnp.int32, (32, LANES), 0)
    unbroken = jnp.ones((32, LANES), F32)
    for n in range(docs.shape[0]):
        begins0 = jnp.where(at == 2 * p, 1.0, begins0)
        begins1 = jnp.where(at == 2 * p + 1, 1.0, begins1)
        unbroken = jnp.where(rows == at // 2, 0.0, unbroken)
        at = at + docs[n]
    goes0, goes1 = 1.0 - begins0, 1.0 - begins1

    tiles = proj.shape[2] // LANES
    sub = lax.broadcasted_iota(jnp.int32, (ORDER, 8, LANES), 1).astype(F32)

    def lane(t):
        return pl.ds(pl.multiple_of(t * LANES, LANES), LANES)

    def head_tile(t, carry):
        d = dec[:, lane(t)]
        lam8 = jnp.exp(-8.0 * d)[:, None, :]
        v = res[:, lane(t)][:, None, :] * jnp.exp(-d[:, None, :] * sub)
        pieces = []
        for k in range(BLK // 8):
            pieces.append(jnp.sum(v, axis=0))
            v = v * lam8
        head[:, lane(t)] = jnp.concatenate(pieces, axis=0)
        for i in range(8):
            dparts[i * tiles + t] = d[2 * i : 2 * i + 2]
        return carry

    lax.fori_loop(0, tiles, head_tile, 0)
    hspec[...] = jnp.dot(fwd[...], split_rows(head[...]), preferred_element_type=F32) * (1.0 / BLK)
    lam256 = jnp.exp(-256.0 * dparts[p])
    for n in range(32):
        through[n] = lam256 * unbroken[n : n + 1, :]

    halo_copy.wait()
    for s in range(3):
        for j in range(2):
            if j == 0:
                before = halo[s, :, :].astype(F32)[8:16]
                before = jnp.where(goes0 > 0.5, before, 0.0)
            else:
                before = proj[s, 112:128, :].astype(F32)[8:16]
                before = jnp.where(goes1 > 0.5, before, 0.0)
            ext[s, j, 0:8, :] = before
            ext[s, j, 8:136, :] = proj[s, j * BLK : (j + 1) * BLK, :].astype(F32)

    def short_tile(t, carry):
        for j in range(2):
            short = []
            for s in range(3):
                total = jnp.zeros((BLK, LANES), F32)
                for tap in range(SHORT):
                    total = total + sf[s, tap : tap + 1, lane(t)] * ext[s, j, 8 - tap : 136 - tap, lane(t)]
                short.append(total)
            query[j, :, lane(t)] = short[0]
            source[:, pl.ds(pl.multiple_of(j * tiles * LANES + t * LANES, LANES), LANES)] = short[1] * short[2]
        return carry

    lax.fori_loop(0, tiles, short_tile, 0)

    def end_tile(t, carry):
        d = dec[:, lane(t)]
        lam8 = jnp.exp(-8.0 * d)[:, None, :]
        lam128 = jnp.exp(-128.0 * d)
        weight = jnp.exp(-d[:, None, :] * (7.0 - sub))
        own = []
        for j in range(2):
            lanes = pl.ds(pl.multiple_of(j * tiles * LANES + t * LANES, LANES), LANES)
            total = jnp.zeros((ORDER, 8, LANES), F32)
            for k in range(BLK // 8):
                total = total * lam8 + source[8 * k : 8 * k + 8, lanes][None]
            own.append(jnp.sum(total * weight, axis=1))
        ends_own[:, lane(t)] = own[0]
        final = own[1] + lam128 * own[0] * goes1
        for i in range(8):
            parts[i * tiles + t] = final[2 * i : 2 * i + 2]
        return carry

    lax.fori_loop(0, tiles, end_tile, 0)

    def to_all(src, dst, send, recv):
        def one(o, carry):
            to = (p + o) % n_ctx
            remote(src.at[to], dst.at[p], send, recv, to, q).start()
            return carry

        lax.fori_loop(1, n_ctx, one, 0)
        dst[p] = src[p]

    def all_in(buf, sem):
        landed(buf.at[pl.ds(0, 31)], sem)

    to_all(parts, rx, a2a_sem.at[0], a2a_sem.at[1])
    pass_on(0, 1)
    seed = half(1 - y_hi, z, core)
    landed(seed, wr.at[1, 0])
    spread(1, seed)
    spec[...] = jnp.dot(fwd[...], split_rows(source[...]), preferred_element_type=F32)
    all_in(rx, a2a_sem.at[1])

    def scan(n, s):
        back[n] = s
        return s * through[n] + rx[n]

    lax.fori_loop(0, 32, scan, jnp.zeros((2, LANES), F32))
    to_all(back, rx2, a2a_sem.at[2], a2a_sem.at[3])
    pass_on(0, 2)

    chans = proj.shape[2]
    for j in range(2):
        cols = slice(j * chans, (j + 1) * chans)
        s_re, s_im = spec[0:BLK, cols], spec[BLK : 2 * BLK, cols]
        h_re, h_im = hspec[0:BLK, :], hspec[BLK : 2 * BLK, :]
        y_re = s_re * h_re - s_im * h_im
        y_im = s_re * h_im + s_im * h_re
        both = jnp.concatenate([y_re, y_im], axis=0)
        intra[j] = jnp.dot(inv[...], split_rows(both), preferred_element_type=F32)
    pass_on(1, 1)

    all_in(rx2, a2a_sem.at[3])
    for t in range(tiles):
        for i in range(8):
            state[2 * i : 2 * i + 2, t * LANES : (t + 1) * LANES] = rx2[i * tiles + t]

    def hidden_block(j):
        def hidden_tile(t, carry):
            d = dec[:, lane(t)]
            lam8 = jnp.exp(-8.0 * d)[:, None, :]
            entering = state[:, lane(t)] * goes0
            if j == 1:
                entering = (jnp.exp(-128.0 * d) * entering + ends_own[:, lane(t)]) * goes1
            v = (res[:, lane(t)] * entering)[:, None, :] * jnp.exp(-d[:, None, :] * (sub + 1.0))
            pieces = []
            for k in range(BLK // 8):
                pieces.append(jnp.sum(v, axis=0))
                v = v * lam8
            response = intra[j, :, lane(t)] + jnp.concatenate(pieces, axis=0)
            hbuf[q, j * BLK : (j + 1) * BLK, lane(t)] = (query[j, :, lane(t)] * response).astype(BF16)
            return carry

        lax.fori_loop(0, tiles, hidden_tile, 0)

    def piece(b, j):
        return hbuf.at[b, pl.ds(j * BLK, BLK), :]

    def give(idx, b, j, to):
        started(remote(piece(b, j), piece(b, j), hs.at[idx], hr.at[idx], p, to))

    def took(idx, b, j):
        landed(piece(b, j), hr.at[idx])

    for j in range(2):
        hidden_block(j)
        give(0 + j, q, j, q_right)
        give(2 + j, q, j, q_left)
        give(4 + j, q, j, q_y)
    pass_on(0, 3)
    pass_on(1, 2)
    took(0, q_left, 0)
    give(6, q_left, 0, q_right)
    give(8, q_left, 0, q_y)
    took(2, q_right, 0)
    give(9, q_right, 0, q_y)
    took(3, q_right, 1)
    give(7, q_right, 1, q_left)
    took(5, q_y, 1)
    give(10, q_y, 1, q_right)
    give(11, q_y, 1, q_left)
    pass_on(0, 4)
    pass_on(1, 3)
    took(8, q_yleft, 0)
    give(12, q_yleft, 0, q_right)
    took(11, q_yright, 1)
    give(13, q_yright, 1, q_left)
    pass_on(1, 4)

    for plane in range(2):
        hi = hi_of[plane]
        landed(half(hi, z, 1 - core), wr.at[plane, 6])
        for hop in range(1, 5):
            oz = (z + step * hop + 8) % 8
            landed(wbuf.at[hi, oz] if hop < 4 else half(hi, oz, 1 - core), wr.at[plane, 6 + hop])
    took(1, q_left, 1)
    took(4, q_y, 0)
    took(6, q_opp, 0)
    took(7, q_opp, 1)
    took(9, q_yright, 0)
    took(10, q_yleft, 1)

    acc[...] = jnp.zeros_like(acc)

    def project(k, carry):
        m = k % 4
        dx = m + (m // 2) * (1 - 2 * (m % 2))
        b = ((y_lo + k // 4) % 2) * 4 + (x + dx) % 4
        weights = wbuf[b // 4, pl.ds(2 * (b % 4), 2)].reshape(4 * BLK, acc.shape[1])
        acc[...] += jnp.dot(hbuf[b], weights, preferred_element_type=F32)
        return carry

    lax.fori_loop(0, 7, project, 0)
    took(12, q_yopp, 0)
    took(13, q_yopp, 1)
    lax.fori_loop(7, 8, project, 0)
    out[...] = acc[...].astype(BF16)

    for copy in sends:
        copy.wait_send()
    landed(parts.at[pl.ds(0, 31)], a2a_sem.at[0])
    landed(back.at[pl.ds(0, 31)], a2a_sem.at[2])


def shards(fwd, inv, projected, short_filter, residues, decay_rates, doc_blocks, out_weight):
    rows, chans = projected.shape[1:]
    vmem = pl.BlockSpec(memory_space=pltpu.VMEM)
    return pl.pallas_call(
        kernel,
        out_shape=jax.ShapeDtypeStruct((rows, out_weight.shape[1]), BF16),
        in_specs=[vmem] * 4 + [pl.BlockSpec(memory_space=pltpu.SMEM)] + [vmem] * 3,
        out_specs=vmem,
        scratch_shapes=[
            pltpu.VMEM((3, 16, chans), BF16),
            pltpu.VMEM((3, 2, 8 + BLK, chans), F32),
            pltpu.VMEM((2, BLK, chans), F32),
            pltpu.VMEM((BLK, 2 * chans), F32),
            pltpu.VMEM((2 * BLK, 2 * chans), F32),
            pltpu.VMEM((2, BLK, chans), F32),
            pltpu.VMEM((BLK, chans), F32),
            pltpu.VMEM((2 * BLK, chans), F32),
            pltpu.VMEM((32, 2, LANES), F32),
            pltpu.VMEM((32, 2, LANES), F32),
            pltpu.VMEM((32, 2, LANES), F32),
            pltpu.VMEM((32, 2, LANES), F32),
            pltpu.VMEM((32, 2, LANES), F32),
            pltpu.VMEM((32, 2, LANES), F32),
            pltpu.VMEM((ORDER, chans), F32),
            pltpu.VMEM((ORDER, chans), F32),
            pltpu.VMEM((2, 8, 2 * BLK, out_weight.shape[1]), BF16),
            pltpu.VMEM((8, rows, chans), BF16),
            pltpu.VMEM((rows, out_weight.shape[1]), F32),
            pltpu.SemaphoreType.DMA((2,)),
            pltpu.SemaphoreType.DMA((4,)),
            pltpu.SemaphoreType.DMA((2, 11)),
            pltpu.SemaphoreType.DMA((2, 11)),
            pltpu.SemaphoreType.DMA((14,)),
            pltpu.SemaphoreType.DMA((14,)),
        ],
        compiler_params=pltpu.CompilerParams(
            collective_id=0, has_side_effects=True, vmem_limit_bytes=40 * 1024 * 1024
        ),
        name="hyena_block",
    )(projected, short_filter, residues, decay_rates, doc_blocks, out_weight, fwd, inv)


def solution(mesh):
    placed = (
        P(None, "ctx", "ch"),
        P(None, None, "ch"),
        P(None, "ch"),
        P(None, "ch"),
        P(),
        P("ctx", "ch"),
    )
    fwd, inv = (jnp.asarray(t) for t in dft_tables())
    return jax.shard_map(
        functools.partial(shards, fwd, inv), mesh=mesh, in_specs=placed, out_specs=P("ctx", "ch"), check_vma=False
    )
```

```python
import functools

import jax
import jax.numpy as jnp
import ml_dtypes
import numpy as np
from jax import lax
from jax.experimental import pallas as pl
from jax.experimental.pallas import tpu as pltpu
from jax.sharding import PartitionSpec as P

ORDER = 16
SHORT = 7
BLK = 128
LANES = 128
MESH = pl.DeviceIdType.MESH
F32, BF16 = jnp.float32, jnp.bfloat16


def dft_tables():
    freq = np.arange(BLK)[:, None] + 0.5
    angles = 2.0 * np.pi * freq * np.arange(BLK)[None, :] / (2 * BLK)
    table = np.concatenate([np.cos(angles), np.sin(angles)], axis=0)

    def split(a):
        high = a.astype(ml_dtypes.bfloat16)
        low = (a - high.astype(np.float64)).astype(ml_dtypes.bfloat16)
        return np.concatenate([high, high, low], axis=1)

    return split(table), split(table.T)


def split_rows(a):
    high = a.astype(BF16)
    low = (a - high.astype(F32)).astype(BF16)
    return jnp.concatenate([high, low, high], axis=0)


def kernel(
    proj_in, sf_in, res_in, dec_in, docs_in, w, fwd_in, inv_in, out,
    proj, sf, res, dec, docs, fwd, inv, halo, ext, query, source, spec, intra, head, hspec,
    parts, rx, back, state, through, ends_own,
    wbuf, hbuf, acc, outv,
    in_sem, halo_sem, out_send, out_recv, back_send, back_recv, ws, wr, hs, hr, done,
):
    p, q = lax.axis_index("ctx"), lax.axis_index("ch")
    n_ctx = lax.axis_size("ctx")
    core = p % 2
    z = (p // 2) % 8
    y_hi = p // 16
    x, y_lo = q % 4, q // 4

    def ctx_of(hi, zz, cc):
        return hi * 16 + zz * 2 + cc

    q_right = y_lo * 4 + (x + 1) % 4
    q_left = y_lo * 4 + (x + 3) % 4
    q_opp = y_lo * 4 + (x + 2) % 4
    q_y = (1 - y_lo) * 4 + x
    q_yright = (1 - y_lo) * 4 + (x + 1) % 4
    q_yleft = (1 - y_lo) * 4 + (x + 3) % 4
    q_yopp = (1 - y_lo) * 4 + (x + 2) % 4

    def remote(src, dst, send, recv, to_ctx, to_ch):
        return pltpu.make_async_remote_copy(
            src_ref=src, dst_ref=dst, send_sem=send, recv_sem=recv,
            device_id=(to_ctx, to_ch), device_id_type=MESH,
        )

    pairs = ((proj_in, proj), (sf_in, sf), (res_in, res), (dec_in, dec), (docs_in, docs), (fwd_in, fwd), (inv_in, inv))
    loads = [pltpu.make_async_copy(src, dst, in_sem.at[i]) for i, (src, dst) in enumerate(pairs)]
    hi_own = pl.ds(core * 128, 128)
    loads.append(pltpu.make_async_copy(w, wbuf.at[y_hi, z, hi_own, :], in_sem.at[len(pairs)]))
    for load in loads:
        load.start()

    group = p // 8
    scans = z < 4
    serves = 2 * y_hi + core
    tile = z % 4

    def scanner(i):
        return (i // 8) * 16 + (i % 4) * 2 + (i // 4) % 2

    barrier = pltpu.get_barrier_semaphore()

    def greet(to_ctx, to_ch):
        pl.semaphore_signal(barrier, inc=1, device_id=(to_ctx, to_ch), device_id_type=MESH)

    greet((p + n_ctx - 1) % n_ctx, q)
    toward = (z - (1 - 2 * core) + 8) % 8
    for c in range(2):
        greet(ctx_of(y_hi, toward, c), q)
    greet(ctx_of(y_hi, z, 1 - core), q)
    greet(ctx_of(1 - y_hi, z, core), q)
    for to in (q_right, q_left, q_y):
        greet(p, to)

    def greet_scanner(i, carry):
        @pl.when(scanner(i) != p)
        def _():
            greet(scanner(i), q)

        return carry

    lax.fori_loop(4 * group, 4 * group + 4, greet_scanner, 0)

    @pl.when(scans)
    def _():
        def greet_member(n, carry):
            @pl.when(n != p)
            def _():
                greet(n, q)

            return carry

        lax.fori_loop(0, 8 * serves + 8, greet_member, 0)

    own_scan = jnp.where(scans, 1, 0)
    pl.semaphore_wait(barrier, 8 + (16 - 4 * group - own_scan) + own_scan * (7 + core))

    halo_copy = remote(
        proj_in.at[:, pl.ds(240, 16), :], halo, halo_sem.at[0], halo_sem.at[1], (p + 1) % n_ctx, q
    )
    halo_copy.start()

    step = 1 - 2 * core
    z_next = (z + step + 8) % 8
    hi_of = (y_hi, 1 - y_hi)
    sends = []

    def started(copy):
        copy.start()
        sends.append(copy)

    def half(hi, zz, cc):
        return wbuf.at[hi, zz, pl.ds(cc * 128, 128), :]

    def spread(plane, src):
        hi = hi_of[plane]
        dst = half(hi, z, core)
        started(remote(src, dst, ws.at[plane, 1], wr.at[plane, 1 + core], ctx_of(y_hi, (z + 1) % 8, 0), q))
        started(remote(src, dst, ws.at[plane, 2], wr.at[plane, 1 + core], ctx_of(y_hi, (z + 7) % 8, 1), q))
        started(remote(src, dst, ws.at[plane, 6], wr.at[plane, 6], ctx_of(y_hi, z, 1 - core), q))

    def landed(ref, sem):
        pltpu.make_async_copy(ref, ref, sem).wait()

    def pass_on(plane, hop):
        hi = hi_of[plane]
        oz = (z - step * hop + 8) % 8
        whole = wbuf.at[hi, oz]
        mine = half(hi, oz, core)
        if hop == 1:
            landed(half(hi, oz, 0), wr.at[plane, 1])
            landed(half(hi, oz, 1), wr.at[plane, 2])
        elif hop < 4:
            landed(whole, wr.at[plane, 1 + hop])
        else:
            landed(mine, wr.at[plane, 5])
        if hop < 3:
            started(remote(whole, whole, ws.at[plane, 2 + hop], wr.at[plane, 2 + hop], ctx_of(y_hi, z_next, core), q))
        elif hop == 3:
            started(remote(mine, mine, ws.at[plane, 5], wr.at[plane, 5], ctx_of(y_hi, z_next, core), q))
        part = whole if hop < 4 else mine
        started(remote(part, part, ws.at[plane, 6 + hop], wr.at[plane, 6 + hop], ctx_of(y_hi, z, 1 - core), q))

    spread(0, w)
    started(
        remote(w, half(y_hi, z, core), ws.at[1, 0], wr.at[1, 0], ctx_of(1 - y_hi, z, core), q)
    )
    for load in loads:
        load.wait()

    begins0, begins1, at = jnp.float32(0), jnp.float32(0), jnp.int32(0)
    rows = lax.broadcasted_iota(jnp.int32, (32, LANES), 0)
    unbroken = jnp.ones((32, LANES), F32)
    for n in range(docs.shape[0]):
        begins0 = jnp.where(at == 2 * p, 1.0, begins0)
        begins1 = jnp.where(at == 2 * p + 1, 1.0, begins1)
        unbroken = jnp.where(rows == at // 2, 0.0, unbroken)
        at = at + docs[n]
    goes0, goes1 = 1.0 - begins0, 1.0 - begins1

    tiles = proj.shape[2] // LANES
    sub = lax.broadcasted_iota(jnp.int32, (ORDER, 8, LANES), 1).astype(F32)

    def lane(t):
        return pl.ds(pl.multiple_of(t * LANES, LANES), LANES)

    def wide(a):
        return jnp.broadcast_to(a[:, None, :], (ORDER, 8, LANES))

    def head_tile(t, carry):
        d = dec[:, lane(t)]
        lam8 = wide(jnp.exp(-8.0 * d))
        v = wide(res[:, lane(t)]) * jnp.exp(-d[:, None, :] * sub)
        pieces = []
        for k in range(BLK // 8):
            pieces.append(jnp.sum(v, axis=0))
            v = v * lam8
        head[:, lane(t)] = jnp.concatenate(pieces, axis=0)
        return carry

    lax.fori_loop(0, tiles, head_tile, 0)
    hspec[...] = jnp.dot(fwd[...], split_rows(head[...]), preferred_element_type=F32) * (1.0 / BLK)
    lam256 = jnp.exp(-256.0 * dec[:, lane(tile)])
    for n in range(32):
        through[n] = lam256 * unbroken[n : n + 1, :]

    def extend(s):
        for j in range(2):
            if j == 0:
                before = halo[s, :, :].astype(F32)[8:16]
                before = jnp.where(goes0 > 0.5, before, 0.0)
            else:
                before = proj[s, 112:128, :].astype(F32)[8:16]
                before = jnp.where(goes1 > 0.5, before, 0.0)
            ext[s, j, 0:8, :] = before
            ext[s, j, 8:136, :] = proj[s, j * BLK : (j + 1) * BLK, :].astype(F32)

    def short(s, j, t):
        total = jnp.zeros((BLK, LANES), F32)
        for tap in range(SHORT):
            total = total + sf[s, tap : tap + 1, lane(t)] * ext[s, j, 8 - tap : 136 - tap, lane(t)]
        return total

    def both_lanes(j, t):
        return pl.ds(pl.multiple_of(j * tiles * LANES + t * LANES, LANES), LANES)

    def source_tile(t, carry):
        for j in range(2):
            source[:, both_lanes(j, t)] = short(1, j, t) * short(2, j, t)
        return carry

    def query_tile(t, carry):
        for j in range(2):
            query[j, :, lane(t)] = short(0, j, t)
        return carry

    halo_copy.wait()
    extend(1)
    extend(2)
    lax.fori_loop(0, tiles, source_tile, 0)

    def end_tile(t, carry):
        d = dec[:, lane(t)]
        lam8 = wide(jnp.exp(-8.0 * d))
        lam128 = jnp.exp(-128.0 * d)
        weight = jnp.exp(-d[:, None, :] * (7.0 - sub))
        own = []
        for j in range(2):
            lanes = both_lanes(j, t)
            total = jnp.zeros((ORDER, 8, LANES), F32)
            for k in range(BLK // 8):
                total = total * lam8 + source[8 * k : 8 * k + 8, lanes][None]
            own.append(jnp.sum(total * weight, axis=1))
        ends_own[:, lane(t)] = own[0]
        final = own[1] + lam128 * own[0] * goes1
        parts[t] = final
        return carry

    lax.fori_loop(0, tiles, end_tile, 0)

    def hand_out(i, carry):
        @pl.when(scanner(i) != p)
        def _():
            remote(parts.at[i % 4], rx.at[p], out_send.at[i], out_recv.at[group], scanner(i), q).start()

        return carry

    lax.fori_loop(4 * group, 16, hand_out, 0)

    seed = half(1 - y_hi, z, core)
    landed(seed, wr.at[1, 0])
    spread(1, seed)
    pass_on(0, 1)
    extend(0)
    lax.fori_loop(0, tiles, query_tile, 0)
    spec[...] = jnp.dot(fwd[...], split_rows(source[...]), preferred_element_type=F32)

    @pl.when(scans)
    def _():
        rx[p] = parts[tile]

        def earlier(g, s):
            landed(rx.at[pl.ds(0, 8)], out_recv.at[g])
            for n in range(8):
                s = s * through[8 * g + n] + rx[8 * g + n]
            return s

        s = lax.fori_loop(0, group, earlier, jnp.zeros((ORDER, LANES), F32))
        landed(rx.at[pl.ds(0, 7)], out_recv.at[group])

        def own_group(g, s):
            for n in range(8):
                s = s * through[8 * g + n] + rx[8 * g + n]
            return s

        s = lax.fori_loop(group, group + core, own_group, s)

        @pl.when(core == 1)
        def _():
            landed(rx.at[pl.ds(0, 8)], out_recv.at[serves])

        for n in range(8):
            back[n] = s
            if n < 7:
                s = s * through[8 * serves + n] + rx[8 * serves + n]
        for n in range(8):

            @pl.when(8 * serves + n != p)
            def _():
                remote(back.at[n], state.at[tile], back_send.at[n], back_recv.at[0], 8 * serves + n, q).start()

        @pl.when(core == 0)
        def _():
            state[tile] = back[p % 8]

    pass_on(1, 1)

    chans = proj.shape[2]
    for j in range(2):
        cols = slice(j * chans, (j + 1) * chans)
        s_re, s_im = spec[0:BLK, cols], spec[BLK : 2 * BLK, cols]
        h_re, h_im = hspec[0:BLK, :], hspec[BLK : 2 * BLK, :]
        y_re = s_re * h_re - s_im * h_im
        y_im = s_re * h_im + s_im * h_re
        both = jnp.concatenate([y_re, y_im], axis=0)
        intra[j] = jnp.dot(inv[...], split_rows(both), preferred_element_type=F32)
    pass_on(0, 2)

    own_part = jnp.logical_and(scans, core == 0)

    @pl.when(own_part)
    def _():
        landed(state.at[pl.ds(0, 3)], back_recv.at[0])

    @pl.when(jnp.logical_not(own_part))
    def _():
        landed(state, back_recv.at[0])

    def hidden_block(j):
        def hidden_tile(t, carry):
            d = dec[:, lane(t)]
            lam8 = wide(jnp.exp(-8.0 * d))
            entering = state[t] * goes0
            if j == 1:
                entering = (jnp.exp(-128.0 * d) * entering + ends_own[:, lane(t)]) * goes1
            v = wide(res[:, lane(t)] * entering) * jnp.exp(-d[:, None, :] * (sub + 1.0))
            pieces = []
            for k in range(BLK // 8):
                pieces.append(jnp.sum(v, axis=0))
                v = v * lam8
            response = intra[j, :, lane(t)] + jnp.concatenate(pieces, axis=0)
            hbuf[q, j * BLK : (j + 1) * BLK, lane(t)] = (query[j, :, lane(t)] * response).astype(BF16)
            return carry

        lax.fori_loop(0, tiles, hidden_tile, 0)

    def piece(b, j):
        return hbuf.at[b, pl.ds(j * BLK, BLK), :]

    def give(idx, b, j, to):
        started(remote(piece(b, j), piece(b, j), hs.at[idx], hr.at[idx], p, to))

    def took(idx, b, j):
        landed(piece(b, j), hr.at[idx])

    for j in range(2):
        hidden_block(j)
        give(0 + j, q, j, q_right)
        give(2 + j, q, j, q_left)
        give(4 + j, q, j, q_y)
    pass_on(1, 2)
    took(0, q_left, 0)
    give(6, q_left, 0, q_right)
    give(8, q_left, 0, q_y)
    took(2, q_right, 0)
    give(9, q_right, 0, q_y)
    pass_on(0, 3)
    took(3, q_right, 1)
    give(7, q_right, 1, q_left)
    took(5, q_y, 1)
    give(10, q_y, 1, q_right)
    give(11, q_y, 1, q_left)
    pass_on(1, 3)
    pass_on(0, 4)
    took(8, q_yleft, 0)
    give(12, q_yleft, 0, q_right)
    took(11, q_yright, 1)
    give(13, q_yright, 1, q_left)
    pass_on(1, 4)

    for plane in range(2):
        hi = hi_of[plane]
        landed(half(hi, z, 1 - core), wr.at[plane, 6])
        for hop in range(1, 5):
            oz = (z + step * hop + 8) % 8
            landed(wbuf.at[hi, oz] if hop < 4 else half(hi, oz, 1 - core), wr.at[plane, 6 + hop])

    def product(b):
        weights = wbuf[b // 4, pl.ds(2 * (b % 4), 2)].reshape(4 * BLK, acc.shape[1])
        return jnp.dot(hbuf[b], weights, preferred_element_type=F32)

    def project(k, carry):
        m = k % 4
        dx = m + (m // 2) * (1 - 2 * (m % 2))
        acc[...] += product(((y_lo + k // 4) % 2) * 4 + (x + dx) % 4)
        return carry

    took(1, q_left, 1)
    took(4, q_y, 0)
    acc[...] = product(q_y)
    lax.fori_loop(0, 3, project, 0)
    took(6, q_opp, 0)
    took(7, q_opp, 1)
    lax.fori_loop(3, 4, project, 0)
    took(9, q_yright, 0)
    took(10, q_yleft, 1)
    lax.fori_loop(5, 7, project, 0)
    took(12, q_yopp, 0)
    took(13, q_yopp, 1)
    outv[...] = (acc[...] + product(q_yopp)).astype(BF16)
    result = pltpu.make_async_copy(outv, out, done.at[0])
    result.start()

    for copy in sends:
        copy.wait_send()

    def handed_out(i, carry):
        @pl.when(scanner(i) != p)
        def _():
            landed(parts.at[i % 4], out_send.at[i])

        return carry

    lax.fori_loop(4 * group, 16, handed_out, 0)

    @pl.when(scans)
    def _():
        for n in range(8):

            @pl.when(8 * serves + n != p)
            def _():
                landed(back.at[n], back_send.at[n])

    result.wait()


def shards(fwd, inv, projected, short_filter, residues, decay_rates, doc_blocks, out_weight):
    rows, chans = projected.shape[1:]
    hbm = pl.BlockSpec(memory_space=pltpu.HBM)
    return pl.pallas_call(
        kernel,
        out_shape=jax.ShapeDtypeStruct((rows, out_weight.shape[1]), BF16),
        in_specs=[hbm] * 8,
        out_specs=hbm,
        scratch_shapes=[
            pltpu.VMEM(projected.shape, BF16),
            pltpu.VMEM(short_filter.shape, F32),
            pltpu.VMEM(residues.shape, F32),
            pltpu.VMEM(decay_rates.shape, F32),
            pltpu.SMEM(doc_blocks.shape, jnp.int32),
            pltpu.VMEM(fwd.shape, BF16),
            pltpu.VMEM(inv.shape, BF16),
            pltpu.VMEM((3, 16, chans), BF16),
            pltpu.VMEM((3, 2, 8 + BLK, chans), F32),
            pltpu.VMEM((2, BLK, chans), F32),
            pltpu.VMEM((BLK, 2 * chans), F32),
            pltpu.VMEM((2 * BLK, 2 * chans), F32),
            pltpu.VMEM((2, BLK, chans), F32),
            pltpu.VMEM((BLK, chans), F32),
            pltpu.VMEM((2 * BLK, chans), F32),
            pltpu.VMEM((4, ORDER, LANES), F32),
            pltpu.VMEM((32, ORDER, LANES), F32),
            pltpu.VMEM((8, ORDER, LANES), F32),
            pltpu.VMEM((4, ORDER, LANES), F32),
            pltpu.VMEM((32, ORDER, LANES), F32),
            pltpu.VMEM((ORDER, chans), F32),
            pltpu.VMEM((2, 8, 2 * BLK, out_weight.shape[1]), BF16),
            pltpu.VMEM((8, rows, chans), BF16),
            pltpu.VMEM((rows, out_weight.shape[1]), F32),
            pltpu.VMEM((rows, out_weight.shape[1]), BF16),
            pltpu.SemaphoreType.DMA((8,)),
            pltpu.SemaphoreType.DMA((2,)),
            pltpu.SemaphoreType.DMA((16,)),
            pltpu.SemaphoreType.DMA((4,)),
            pltpu.SemaphoreType.DMA((8,)),
            pltpu.SemaphoreType.DMA((1,)),
            pltpu.SemaphoreType.DMA((2, 11)),
            pltpu.SemaphoreType.DMA((2, 11)),
            pltpu.SemaphoreType.DMA((14,)),
            pltpu.SemaphoreType.DMA((14,)),
            pltpu.SemaphoreType.DMA((1,)),
        ],
        compiler_params=pltpu.CompilerParams(
            collective_id=0, has_side_effects=True, vmem_limit_bytes=60 * 1024 * 1024
        ),
        name="hyena_block",
    )(projected, short_filter, residues, decay_rates, doc_blocks, out_weight, fwd, inv)


def solution(mesh):
    placed = (
        P(None, "ctx", "ch"),
        P(None, None, "ch"),
        P(None, "ch"),
        P(None, "ch"),
        P(),
        P("ctx", "ch"),
    )
    fwd, inv = (jnp.asarray(t) for t in dft_tables())
    return jax.shard_map(
        functools.partial(shards, fwd, inv), mesh=mesh, in_specs=placed, out_specs=P("ctx", "ch"), check_vma=False
    )
```

```python
import functools

import jax
import jax.numpy as jnp
import ml_dtypes
import numpy as np
from jax import lax
from jax.experimental import pallas as pl
from jax.experimental.pallas import tpu as pltpu
from jax.sharding import PartitionSpec as P

ORDER = 16
SHORT = 7
BLK = 128
LANES = 128
MESH = pl.DeviceIdType.MESH
F32, BF16 = jnp.float32, jnp.bfloat16


def dft_tables():
    freq = np.arange(BLK)[:, None] + 0.5
    angles = 2.0 * np.pi * freq * np.arange(BLK)[None, :] / (2 * BLK)
    table = np.concatenate([np.cos(angles), np.sin(angles)], axis=0)

    def split(a):
        high = a.astype(ml_dtypes.bfloat16)
        low = (a - high.astype(np.float64)).astype(ml_dtypes.bfloat16)
        return np.concatenate([high, high, low], axis=1)

    return split(table), split(table.T)


def split_rows(a):
    high = a.astype(BF16)
    low = (a - high.astype(F32)).astype(BF16)
    return jnp.concatenate([high, low, high], axis=0)


def kernel(
    proj_in, sf_in, res_in, dec_in, docs_in, w, fwd_in, inv_in, out,
    proj, sf, res, dec, docs, fwd, inv, halo, ext, query, source, spec, intra, head, hspec,
    parts, rx, back, state, through, ends_own, ends_next, lam8, lam128, first_weight, reach,
    wbuf, hbuf, acc,
    in_sem, halo_sem, out_send, out_recv, back_send, back_recv, ws, wr, hs, hr,
):
    p, q = lax.axis_index("ctx"), lax.axis_index("ch")
    n_ctx = lax.axis_size("ctx")
    core = p % 2
    z = (p // 2) % 8
    y_hi = p // 16
    x, y_lo = q % 4, q // 4

    def ctx_of(hi, zz, cc):
        return hi * 16 + zz * 2 + cc

    q_right = y_lo * 4 + (x + 1) % 4
    q_left = y_lo * 4 + (x + 3) % 4
    q_opp = y_lo * 4 + (x + 2) % 4
    q_y = (1 - y_lo) * 4 + x
    q_yright = (1 - y_lo) * 4 + (x + 1) % 4
    q_yleft = (1 - y_lo) * 4 + (x + 3) % 4
    q_yopp = (1 - y_lo) * 4 + (x + 2) % 4

    def remote(src, dst, send, recv, to_ctx, to_ch):
        return pltpu.make_async_remote_copy(
            src_ref=src, dst_ref=dst, send_sem=send, recv_sem=recv,
            device_id=(to_ctx, to_ch), device_id_type=MESH,
        )

    pairs = ((proj_in, proj), (sf_in, sf), (res_in, res), (dec_in, dec), (docs_in, docs), (fwd_in, fwd), (inv_in, inv))
    loads = [pltpu.make_async_copy(src, dst, in_sem.at[i]) for i, (src, dst) in enumerate(pairs)]
    hi_own = pl.ds(core * 128, 128)
    loads.append(pltpu.make_async_copy(w, wbuf.at[y_hi, z, hi_own, :], in_sem.at[len(pairs)]))
    for load in loads:
        load.start()

    group = p // 8
    scans = z < 4
    serves = 2 * y_hi + core
    tile = z % 4

    def scanner(i):
        return (i // 8) * 16 + (i % 4) * 2 + (i // 4) % 2

    barrier = pltpu.get_barrier_semaphore()

    def greet(to_ctx, to_ch):
        pl.semaphore_signal(barrier, inc=1, device_id=(to_ctx, to_ch), device_id_type=MESH)

    greet((p + n_ctx - 1) % n_ctx, q)
    toward = (z - (1 - 2 * core) + 8) % 8
    for c in range(2):
        greet(ctx_of(y_hi, toward, c), q)
    greet(ctx_of(y_hi, z, 1 - core), q)
    greet(ctx_of(1 - y_hi, z, core), q)
    for to in (q_right, q_left, q_y):
        greet(p, to)

    def greet_scanner(i, carry):
        @pl.when(scanner(i) != p)
        def _():
            greet(scanner(i), q)

        return carry

    lax.fori_loop(4 * group, 4 * group + 4, greet_scanner, 0)

    @pl.when(scans)
    def _():
        def greet_member(n, carry):
            @pl.when(n != p)
            def _():
                greet(n, q)

            return carry

        lax.fori_loop(0, 8 * serves + 8, greet_member, 0)

    own_scan = jnp.where(scans, 1, 0)
    pl.semaphore_wait(barrier, 8 + (16 - 4 * group - own_scan) + own_scan * (7 + core))

    halo_copy = remote(
        proj_in.at[:, pl.ds(240, 16), :], halo, halo_sem.at[0], halo_sem.at[1], (p + 1) % n_ctx, q
    )
    halo_copy.start()

    step = 1 - 2 * core
    z_next = (z + step + 8) % 8
    hi_of = (y_hi, 1 - y_hi)
    sends = []

    def started(copy):
        copy.start()
        sends.append(copy)

    def half(hi, zz, cc):
        return wbuf.at[hi, zz, pl.ds(cc * 128, 128), :]

    def spread(plane, src):
        hi = hi_of[plane]
        dst = half(hi, z, core)
        started(remote(src, dst, ws.at[plane, 1], wr.at[plane, 1 + core], ctx_of(y_hi, (z + 1) % 8, 0), q))
        started(remote(src, dst, ws.at[plane, 2], wr.at[plane, 1 + core], ctx_of(y_hi, (z + 7) % 8, 1), q))
        started(remote(src, dst, ws.at[plane, 6], wr.at[plane, 6], ctx_of(y_hi, z, 1 - core), q))

    def landed(ref, sem):
        pltpu.make_async_copy(ref, ref, sem).wait()

    def pass_on(plane, hop):
        hi = hi_of[plane]
        oz = (z - step * hop + 8) % 8
        whole = wbuf.at[hi, oz]
        mine = half(hi, oz, core)
        if hop == 1:
            landed(half(hi, oz, 0), wr.at[plane, 1])
            landed(half(hi, oz, 1), wr.at[plane, 2])
        elif hop < 4:
            landed(whole, wr.at[plane, 1 + hop])
        else:
            landed(mine, wr.at[plane, 5])
        if hop < 3:
            started(remote(whole, whole, ws.at[plane, 2 + hop], wr.at[plane, 2 + hop], ctx_of(y_hi, z_next, core), q))
        elif hop == 3:
            started(remote(mine, mine, ws.at[plane, 5], wr.at[plane, 5], ctx_of(y_hi, z_next, core), q))
        part = whole if hop < 4 else mine
        started(remote(part, part, ws.at[plane, 6 + hop], wr.at[plane, 6 + hop], ctx_of(y_hi, z, 1 - core), q))

    spread(0, w)
    started(
        remote(w, half(y_hi, z, core), ws.at[1, 0], wr.at[1, 0], ctx_of(1 - y_hi, z, core), q)
    )
    for load in loads:
        load.wait()

    begins0, begins1, at = jnp.float32(0), jnp.float32(0), jnp.int32(0)
    rows = lax.broadcasted_iota(jnp.int32, (32, LANES), 0)
    unbroken = jnp.ones((32, LANES), F32)
    for n in range(docs.shape[0]):
        begins0 = jnp.where(at == 2 * p, 1.0, begins0)
        begins1 = jnp.where(at == 2 * p + 1, 1.0, begins1)
        unbroken = jnp.where(rows == at // 2, 0.0, unbroken)
        at = at + docs[n]
    goes0, goes1 = 1.0 - begins0, 1.0 - begins1

    tiles = proj.shape[2] // LANES
    sub = lax.broadcasted_iota(jnp.int32, (ORDER, 8, LANES), 1).astype(F32)

    def lane(t):
        return pl.ds(pl.multiple_of(t * LANES, LANES), LANES)

    def wide(a):
        return jnp.broadcast_to(a[:, None, :], (ORDER, 8, LANES))

    def wide(a):
        return jnp.broadcast_to(a[:, None, :], (ORDER, 8, LANES))

    def extend(s):
        for j in range(2):
            if j == 1:
                before = proj[s, 112:128, :].astype(F32)[8:16]
                ext[s, j, 0:8, :] = jnp.where(goes1 > 0.5, before, 0.0)
            ext[s, j, 8:136, :] = proj[s, j * BLK : (j + 1) * BLK, :].astype(F32)

    def extend_from_halo(s):
        before = halo[s, :, :].astype(F32)[8:16]
        ext[s, 0, 0:8, :] = jnp.where(goes0 > 0.5, before, 0.0)

    def short(s, j, t, begin, end):
        total = jnp.zeros((end - begin, LANES), F32)
        for tap in range(SHORT):
            total = total + sf[s, tap : tap + 1, lane(t)] * ext[s, j, begin + 8 - tap : end + 8 - tap, lane(t)]
        return total

    def both_lanes(j, t):
        return pl.ds(pl.multiple_of(j * tiles * LANES + t * LANES, LANES), LANES)

    def local_tile(t, carry):
        source[8:BLK, both_lanes(0, t)] = short(1, 0, t, 8, BLK) * short(2, 0, t, 8, BLK)
        source[:, both_lanes(1, t)] = short(1, 1, t, 0, BLK) * short(2, 1, t, 0, BLK)
        d = dec[:, lane(t)]
        step8 = wide(jnp.exp(-8.0 * d))
        lam8[t] = step8
        weight = jnp.exp(-d[:, None, :] * (7.0 - sub))
        for j in range(2):
            total = jnp.zeros((ORDER, 8, LANES), F32)
            for k in range(1 - j, BLK // 8):
                total = total * step8 + source[8 * k : 8 * k + 8, both_lanes(j, t)][None]
            own = jnp.sum(total * weight, axis=1)
            if j == 0:
                ends_own[:, lane(t)] = own
            else:
                ends_next[:, lane(t)] = own
        first_weight[t] = jnp.exp(-d[:, None, :] * (127.0 - sub))
        lam128[:, lane(t)] = jnp.exp(-128.0 * d)
        return carry

    def halo_tile(t, carry):
        first = short(1, 0, t, 0, 8) * short(2, 0, t, 0, 8)
        source[0:8, both_lanes(0, t)] = first
        own = ends_own[:, lane(t)] + jnp.sum(first_weight[t] * first[None], axis=1)
        ends_own[:, lane(t)] = own
        parts[t] = ends_next[:, lane(t)] + lam128[:, lane(t)] * own * goes1
        return carry

    def query_tile(t, carry):
        for j in range(2):
            query[j, :, lane(t)] = short(0, j, t, 0, BLK)
        return carry

    extend(1)
    extend(2)
    lax.fori_loop(0, tiles, local_tile, 0)

    @pl.when(scans)
    def _():
        lam256 = jnp.exp(-256.0 * dec[:, lane(tile)])
        for n in range(32):
            through[n] = lam256 * unbroken[n : n + 1, :]

    halo_copy.wait()
    extend_from_halo(1)
    extend_from_halo(2)
    lax.fori_loop(0, tiles, halo_tile, 0)

    for i in range(16):

        @pl.when(jnp.logical_and(i >= 4 * group, p != scanner(i)))
        def _():
            remote(parts.at[i % 4], rx.at[p], out_send.at[i], out_recv.at[group], scanner(i), q).start()

    seed = half(1 - y_hi, z, core)
    landed(seed, wr.at[1, 0])
    spread(1, seed)
    pass_on(0, 1)
    extend(0)
    extend_from_halo(0)
    lax.fori_loop(0, tiles, query_tile, 0)
    def head_tile(t, carry):
        d = dec[:, lane(t)]
        step8 = lam8[t]
        v = wide(res[:, lane(t)]) * jnp.exp(-d[:, None, :] * sub)
        reach[t] = wide(res[:, lane(t)]) * jnp.exp(-d[:, None, :] * (sub + 1.0))
        pieces = []
        for k in range(BLK // 8):
            pieces.append(jnp.sum(v, axis=0))
            v = v * step8
        head[:, lane(t)] = jnp.concatenate(pieces, axis=0)
        return carry

    lax.fori_loop(0, tiles, head_tile, 0)
    hspec[...] = jnp.dot(fwd[...], split_rows(head[...]), preferred_element_type=F32) * (1.0 / BLK)
    spec[...] = jnp.dot(fwd[...], split_rows(source[...]), preferred_element_type=F32)

    @pl.when(scans)
    def _():
        rx[p] = parts[tile]

        def earlier(g, s):
            landed(rx.at[pl.ds(0, 8)], out_recv.at[g])
            for n in range(8):
                s = s * through[8 * g + n] + rx[8 * g + n]
            return s

        s = lax.fori_loop(0, group, earlier, jnp.zeros((ORDER, LANES), F32))
        landed(rx.at[pl.ds(0, 7)], out_recv.at[group])

        def own_group(g, s):
            for n in range(8):
                s = s * through[8 * g + n] + rx[8 * g + n]
            return s

        s = lax.fori_loop(group, group + core, own_group, s)

        @pl.when(core == 1)
        def _():
            landed(rx.at[pl.ds(0, 8)], out_recv.at[serves])

        for n in range(8):
            back[n] = s
            if n < 7:
                s = s * through[8 * serves + n] + rx[8 * serves + n]
        for n in range(8):

            @pl.when(8 * serves + n != p)
            def _():
                remote(back.at[n], state.at[tile], back_send.at[n], back_recv.at[0], 8 * serves + n, q).start()

        @pl.when(core == 0)
        def _():
            state[tile] = back[p % 8]

    pass_on(1, 1)

    chans = proj.shape[2]
    for j in range(2):
        cols = slice(j * chans, (j + 1) * chans)
        s_re, s_im = spec[0:BLK, cols], spec[BLK : 2 * BLK, cols]
        h_re, h_im = hspec[0:BLK, :], hspec[BLK : 2 * BLK, :]
        y_re = s_re * h_re - s_im * h_im
        y_im = s_re * h_im + s_im * h_re
        both = jnp.concatenate([y_re, y_im], axis=0)
        intra[j] = jnp.dot(inv[...], split_rows(both), preferred_element_type=F32)
    pass_on(0, 2)

    own_part = jnp.logical_and(scans, core == 0)

    @pl.when(own_part)
    def _():
        landed(state.at[pl.ds(0, 3)], back_recv.at[0])

    @pl.when(jnp.logical_not(own_part))
    def _():
        landed(state, back_recv.at[0])

    def hidden_block(j):
        def hidden_tile(t, carry):
            step8 = lam8[t]
            entering = state[t] * goes0
            if j == 1:
                entering = (lam128[:, lane(t)] * entering + ends_own[:, lane(t)]) * goes1
            v = wide(entering) * reach[t]
            pieces = []
            for k in range(BLK // 8):
                pieces.append(jnp.sum(v, axis=0))
                v = v * step8
            response = intra[j, :, lane(t)] + jnp.concatenate(pieces, axis=0)
            hbuf[q, j * BLK : (j + 1) * BLK, lane(t)] = (query[j, :, lane(t)] * response).astype(BF16)
            return carry

        lax.fori_loop(0, tiles, hidden_tile, 0)

    def piece(b, j):
        return hbuf.at[b, pl.ds(j * BLK, BLK), :]

    def give(idx, b, j, to):
        started(remote(piece(b, j), piece(b, j), hs.at[idx], hr.at[idx], p, to))

    def took(idx, b, j):
        landed(piece(b, j), hr.at[idx])

    hidden_block(0)
    give(0, q, 0, q_right)
    hidden_block(1)
    give(3, q, 1, q_left)
    give(5, q, 1, q_y)
    give(1, q, 1, q_right)
    give(2, q, 0, q_left)
    give(4, q, 0, q_y)
    pass_on(1, 2)
    took(0, q_left, 0)
    give(6, q_left, 0, q_right)
    give(8, q_left, 0, q_y)
    took(5, q_y, 1)
    give(11, q_y, 1, q_left)
    give(10, q_y, 1, q_right)
    took(3, q_right, 1)
    give(7, q_right, 1, q_left)
    pass_on(0, 3)
    took(2, q_right, 0)
    give(9, q_right, 0, q_y)
    pass_on(1, 3)
    took(8, q_yleft, 0)
    give(12, q_yleft, 0, q_right)
    took(11, q_yright, 1)
    give(13, q_yright, 1, q_left)
    pass_on(0, 4)
    pass_on(1, 4)

    for plane in range(2):
        hi = hi_of[plane]
        landed(half(hi, z, 1 - core), wr.at[plane, 6])
        for hop in range(1, 5):
            oz = (z + step * hop + 8) % 8
            landed(wbuf.at[hi, oz] if hop < 4 else half(hi, oz, 1 - core), wr.at[plane, 6 + hop])

    def product(b):
        weights = wbuf[b // 4, pl.ds(2 * (b % 4), 2)].reshape(4 * BLK, acc.shape[1])
        return jnp.dot(hbuf[b], weights, preferred_element_type=F32)

    def project(k, carry):
        m = k % 4
        dx = m + (m // 2) * (1 - 2 * (m % 2))
        acc[...] += product(((y_lo + k // 4) % 2) * 4 + (x + dx) % 4)
        return carry

    took(1, q_left, 1)
    took(4, q_y, 0)
    acc[...] = product(q_y)
    lax.fori_loop(0, 3, project, 0)
    took(6, q_opp, 0)
    took(7, q_opp, 1)
    lax.fori_loop(3, 4, project, 0)
    took(9, q_yright, 0)
    took(10, q_yleft, 1)
    lax.fori_loop(5, 7, project, 0)
    took(12, q_yopp, 0)
    took(13, q_yopp, 1)
    out[...] = (acc[...] + product(q_yopp)).astype(BF16)

    for copy in sends:
        copy.wait_send()

    def handed_out(i, carry):
        @pl.when(scanner(i) != p)
        def _():
            landed(parts.at[i % 4], out_send.at[i])

        return carry

    lax.fori_loop(4 * group, 16, handed_out, 0)

    @pl.when(scans)
    def _():
        for n in range(8):

            @pl.when(8 * serves + n != p)
            def _():
                landed(back.at[n], back_send.at[n])


def shards(fwd, inv, projected, short_filter, residues, decay_rates, doc_blocks, out_weight):
    rows, chans = projected.shape[1:]
    hbm = pl.BlockSpec(memory_space=pltpu.HBM)
    return pl.pallas_call(
        kernel,
        out_shape=pltpu.VMEM((rows, out_weight.shape[1]), BF16),
        in_specs=[hbm] * 8,
        out_specs=pl.BlockSpec(memory_space=pltpu.VMEM),
        scratch_shapes=[
            pltpu.VMEM(projected.shape, BF16),
            pltpu.VMEM(short_filter.shape, F32),
            pltpu.VMEM(residues.shape, F32),
            pltpu.VMEM(decay_rates.shape, F32),
            pltpu.SMEM(doc_blocks.shape, jnp.int32),
            pltpu.VMEM(fwd.shape, BF16),
            pltpu.VMEM(inv.shape, BF16),
            pltpu.VMEM((3, 16, chans), BF16),
            pltpu.VMEM((3, 2, 8 + BLK, chans), F32),
            pltpu.VMEM((2, BLK, chans), F32),
            pltpu.VMEM((BLK, 2 * chans), F32),
            pltpu.VMEM((2 * BLK, 2 * chans), F32),
            pltpu.VMEM((2, BLK, chans), F32),
            pltpu.VMEM((BLK, chans), F32),
            pltpu.VMEM((2 * BLK, chans), F32),
            pltpu.VMEM((4, ORDER, LANES), F32),
            pltpu.VMEM((32, ORDER, LANES), F32),
            pltpu.VMEM((8, ORDER, LANES), F32),
            pltpu.VMEM((4, ORDER, LANES), F32),
            pltpu.VMEM((32, ORDER, LANES), F32),
            pltpu.VMEM((ORDER, chans), F32),
            pltpu.VMEM((ORDER, chans), F32),
            pltpu.VMEM((4, ORDER, 8, LANES), F32),
            pltpu.VMEM((ORDER, chans), F32),
            pltpu.VMEM((4, ORDER, 8, LANES), F32),
            pltpu.VMEM((4, ORDER, 8, LANES), F32),
            pltpu.VMEM((2, 8, 2 * BLK, out_weight.shape[1]), BF16),
            pltpu.VMEM((8, rows, chans), BF16),
            pltpu.VMEM((rows, out_weight.shape[1]), F32),
            pltpu.SemaphoreType.DMA((8,)),
            pltpu.SemaphoreType.DMA((2,)),
            pltpu.SemaphoreType.DMA((16,)),
            pltpu.SemaphoreType.DMA((4,)),
            pltpu.SemaphoreType.DMA((8,)),
            pltpu.SemaphoreType.DMA((1,)),
            pltpu.SemaphoreType.DMA((2, 11)),
            pltpu.SemaphoreType.DMA((2, 11)),
            pltpu.SemaphoreType.DMA((14,)),
            pltpu.SemaphoreType.DMA((14,)),
        ],
        compiler_params=pltpu.CompilerParams(
            collective_id=0, has_side_effects=True, vmem_limit_bytes=60 * 1024 * 1024
        ),
        name="hyena_block",
    )(projected, short_filter, residues, decay_rates, doc_blocks, out_weight, fwd, inv)


def solution(mesh):
    placed = (
        P(None, "ctx", "ch"),
        P(None, None, "ch"),
        P(None, "ch"),
        P(None, "ch"),
        P(),
        P("ctx", "ch"),
    )
    fwd, inv = (jnp.asarray(t) for t in dft_tables())
    return jax.shard_map(
        functools.partial(shards, fwd, inv), mesh=mesh, in_specs=placed, out_specs=P("ctx", "ch"), check_vma=False
    )
```

```python
import functools

import jax
import jax.numpy as jnp
import ml_dtypes
import numpy as np
from jax import lax
from jax.experimental import pallas as pl
from jax.experimental.pallas import tpu as pltpu
from jax.sharding import PartitionSpec as P

ORDER = 16
SHORT = 7
BLK = 128
LANES = 128
MESH = pl.DeviceIdType.MESH
F32, BF16 = jnp.float32, jnp.bfloat16


def dft_tables():
    freq = np.arange(BLK)[:, None] + 0.5
    angles = 2.0 * np.pi * freq * np.arange(BLK)[None, :] / (2 * BLK)
    table = np.concatenate([np.cos(angles), np.sin(angles)], axis=0)

    def split(a):
        high = a.astype(ml_dtypes.bfloat16)
        low = (a - high.astype(np.float64)).astype(ml_dtypes.bfloat16)
        return np.concatenate([high, high, low], axis=1)

    return split(table), split(table.T)


def split_rows(a):
    high = a.astype(BF16)
    low = (a - high.astype(F32)).astype(BF16)
    return jnp.concatenate([high, low, high], axis=0)


def kernel(
    proj_in, sf_in, res_in, dec_in, docs_in, w, fwd_in, inv_in, out,
    proj, sf, res, dec, docs, fwd, inv, halo, ext, query, source, spec, intra, head, hspec,
    parts, rx, back, state, through, ends_own, ends_next, lam8, lam128, first_weight, reach,
    wbuf, hbuf, acc,
    in_sem, halo_sem, out_send, out_recv, back_send, back_recv, ws, wr, hs, hr,
):
    p, q = lax.axis_index("ctx"), lax.axis_index("ch")
    n_ctx = lax.axis_size("ctx")
    core = p % 2
    z = (p // 2) % 8
    y_hi = p // 16
    x, y_lo = q % 4, q // 4

    def ctx_of(hi, zz, cc):
        return hi * 16 + zz * 2 + cc

    q_right = y_lo * 4 + (x + 1) % 4
    q_left = y_lo * 4 + (x + 3) % 4
    q_opp = y_lo * 4 + (x + 2) % 4
    q_y = (1 - y_lo) * 4 + x
    q_yright = (1 - y_lo) * 4 + (x + 1) % 4
    q_yleft = (1 - y_lo) * 4 + (x + 3) % 4
    q_yopp = (1 - y_lo) * 4 + (x + 2) % 4

    def remote(src, dst, send, recv, to_ctx, to_ch):
        return pltpu.make_async_remote_copy(
            src_ref=src, dst_ref=dst, send_sem=send, recv_sem=recv,
            device_id=(to_ctx, to_ch), device_id_type=MESH,
        )

    pairs = ((proj_in, proj), (sf_in, sf), (res_in, res), (dec_in, dec), (docs_in, docs), (fwd_in, fwd), (inv_in, inv))
    loads = [pltpu.make_async_copy(src, dst, in_sem.at[i]) for i, (src, dst) in enumerate(pairs)]
    hi_own = pl.ds(core * 128, 128)
    loads.append(pltpu.make_async_copy(w, wbuf.at[y_hi, z, hi_own, :], in_sem.at[len(pairs)]))
    for load in loads:
        load.start()

    group = p // 8
    scans = z < 4
    serves = 2 * y_hi + core
    tile = z % 4

    def scanner(i):
        return (i // 8) * 16 + (i % 4) * 2 + (i // 4) % 2

    barrier = pltpu.get_barrier_semaphore()

    def greet(to_ctx, to_ch):
        pl.semaphore_signal(barrier, inc=1, device_id=(to_ctx, to_ch), device_id_type=MESH)

    greet((p + n_ctx - 1) % n_ctx, q)
    toward = (z - (1 - 2 * core) + 8) % 8
    for c in range(2):
        greet(ctx_of(y_hi, toward, c), q)
    greet(ctx_of(y_hi, z, 1 - core), q)
    greet(ctx_of(1 - y_hi, z, core), q)
    for to in (q_right, q_left, q_y):
        greet(p, to)

    def greet_scanner(i, carry):
        @pl.when(scanner(i) != p)
        def _():
            greet(scanner(i), q)

        return carry

    lax.fori_loop(4 * group, 4 * group + 4, greet_scanner, 0)

    @pl.when(scans)
    def _():
        def greet_member(n, carry):
            @pl.when(n != p)
            def _():
                greet(n, q)

            return carry

        lax.fori_loop(0, 8 * serves + 8, greet_member, 0)

    own_scan = jnp.where(scans, 1, 0)
    pl.semaphore_wait(barrier, 8 + (16 - 4 * group - own_scan) + own_scan * (7 + core))

    halo_copy = remote(
        proj_in.at[:, pl.ds(240, 16), :], halo, halo_sem.at[0], halo_sem.at[1], (p + 1) % n_ctx, q
    )
    halo_copy.start()

    step = 1 - 2 * core
    z_next = (z + step + 8) % 8
    hi_of = (y_hi, 1 - y_hi)
    sends = []

    def started(copy):
        copy.start()
        sends.append(copy)

    def half(hi, zz, cc):
        return wbuf.at[hi, zz, pl.ds(cc * 128, 128), :]

    def spread(plane, src):
        hi = hi_of[plane]
        dst = half(hi, z, core)
        started(remote(src, dst, ws.at[plane, 1], wr.at[plane, 1 + core], ctx_of(y_hi, (z + 1) % 8, 0), q))
        started(remote(src, dst, ws.at[plane, 2], wr.at[plane, 1 + core], ctx_of(y_hi, (z + 7) % 8, 1), q))
        started(remote(src, dst, ws.at[plane, 6], wr.at[plane, 6], ctx_of(y_hi, z, 1 - core), q))

    def landed(ref, sem):
        pltpu.make_async_copy(ref, ref, sem).wait()

    def pass_on(plane, hop):
        hi = hi_of[plane]
        oz = (z - step * hop + 8) % 8
        whole = wbuf.at[hi, oz]
        mine = half(hi, oz, core)
        if hop == 1:
            landed(half(hi, oz, 0), wr.at[plane, 1])
            landed(half(hi, oz, 1), wr.at[plane, 2])
        elif hop < 4:
            landed(whole, wr.at[plane, 1 + hop])
        else:
            landed(mine, wr.at[plane, 5])
        if hop < 3:
            started(remote(whole, whole, ws.at[plane, 2 + hop], wr.at[plane, 2 + hop], ctx_of(y_hi, z_next, core), q))
        elif hop == 3:
            started(remote(mine, mine, ws.at[plane, 5], wr.at[plane, 5], ctx_of(y_hi, z_next, core), q))
        part = whole if hop < 4 else mine
        started(remote(part, part, ws.at[plane, 6 + hop], wr.at[plane, 6 + hop], ctx_of(y_hi, z, 1 - core), q))

    spread(0, w)
    started(
        remote(w, half(y_hi, z, core), ws.at[1, 0], wr.at[1, 0], ctx_of(1 - y_hi, z, core), q)
    )
    for load in loads:
        load.wait()

    begins0, begins1, at = jnp.float32(0), jnp.float32(0), jnp.int32(0)
    rows = lax.broadcasted_iota(jnp.int32, (32, LANES), 0)
    unbroken = jnp.ones((32, LANES), F32)
    for n in range(docs.shape[0]):
        begins0 = jnp.where(at == 2 * p, 1.0, begins0)
        begins1 = jnp.where(at == 2 * p + 1, 1.0, begins1)
        unbroken = jnp.where(rows == at // 2, 0.0, unbroken)
        at = at + docs[n]
    goes0, goes1 = 1.0 - begins0, 1.0 - begins1

    tiles = proj.shape[2] // LANES
    sub = lax.broadcasted_iota(jnp.int32, (ORDER, 8, LANES), 1).astype(F32)

    def lane(t):
        return pl.ds(pl.multiple_of(t * LANES, LANES), LANES)

    def wide(a):
        return jnp.broadcast_to(a[:, None, :], (ORDER, 8, LANES))

    def wide(a):
        return jnp.broadcast_to(a[:, None, :], (ORDER, 8, LANES))

    def extend(s):
        for j in range(2):
            if j == 1:
                before = proj[s, 112:128, :].astype(F32)[8:16]
                ext[s, j, 0:8, :] = jnp.where(goes1 > 0.5, before, 0.0)
            ext[s, j, 8:136, :] = proj[s, j * BLK : (j + 1) * BLK, :].astype(F32)

    def extend_from_halo(s):
        before = halo[s, :, :].astype(F32)[8:16]
        ext[s, 0, 0:8, :] = jnp.where(goes0 > 0.5, before, 0.0)

    def short(s, j, t, begin, end):
        total = jnp.zeros((end - begin, LANES), F32)
        for tap in range(SHORT):
            total = total + sf[s, tap : tap + 1, lane(t)] * ext[s, j, begin + 8 - tap : end + 8 - tap, lane(t)]
        return total

    def both_lanes(j, t):
        return pl.ds(pl.multiple_of(j * tiles * LANES + t * LANES, LANES), LANES)

    def local_tile(t, carry):
        source[8:BLK, both_lanes(0, t)] = short(1, 0, t, 8, BLK) * short(2, 0, t, 8, BLK)
        source[:, both_lanes(1, t)] = short(1, 1, t, 0, BLK) * short(2, 1, t, 0, BLK)
        d = dec[:, lane(t)]
        step8 = wide(jnp.exp(-8.0 * d))
        lam8[t] = step8
        weight = jnp.exp(-d[:, None, :] * (7.0 - sub))
        for j in range(2):
            total = jnp.zeros((ORDER, 8, LANES), F32)
            for k in range(1 - j, BLK // 8):
                total = total * step8 + source[8 * k : 8 * k + 8, both_lanes(j, t)][None]
            own = jnp.sum(total * weight, axis=1)
            if j == 0:
                ends_own[:, lane(t)] = own
            else:
                ends_next[:, lane(t)] = own
        first_weight[t] = jnp.exp(-d[:, None, :] * (127.0 - sub))
        lam128[:, lane(t)] = jnp.exp(-128.0 * d)
        return carry

    def halo_tile(t, carry):
        first = short(1, 0, t, 0, 8) * short(2, 0, t, 0, 8)
        source[0:8, both_lanes(0, t)] = first
        own = ends_own[:, lane(t)] + jnp.sum(first_weight[t] * first[None], axis=1)
        ends_own[:, lane(t)] = own
        parts[t] = ends_next[:, lane(t)] + lam128[:, lane(t)] * own * goes1
        return carry

    def query_tile(t, carry):
        for j in range(2):
            query[j, :, lane(t)] = short(0, j, t, 0, BLK)
        return carry

    extend(1)
    extend(2)
    lax.fori_loop(0, tiles, local_tile, 0)

    @pl.when(scans)
    def _():
        lam256 = jnp.exp(-256.0 * dec[:, lane(tile)])
        for n in range(32):
            through[n] = lam256 * unbroken[n : n + 1, :]

    halo_copy.wait()
    extend_from_halo(1)
    extend_from_halo(2)
    lax.fori_loop(0, tiles, halo_tile, 0)

    for i in range(16):

        @pl.when(jnp.logical_and(i >= 4 * group, p != scanner(i)))
        def _():
            remote(parts.at[i % 4], rx.at[p], out_send.at[i], out_recv.at[group], scanner(i), q).start()

    seed = half(1 - y_hi, z, core)
    landed(seed, wr.at[1, 0])
    spread(1, seed)
    pass_on(0, 1)
    extend(0)
    extend_from_halo(0)
    lax.fori_loop(0, tiles, query_tile, 0)
    def head_tile(t, carry):
        d = dec[:, lane(t)]
        step8 = lam8[t]
        v = wide(res[:, lane(t)]) * jnp.exp(-d[:, None, :] * sub)
        reach[t] = wide(res[:, lane(t)]) * jnp.exp(-d[:, None, :] * (sub + 1.0))
        pieces = []
        for k in range(BLK // 8):
            pieces.append(jnp.sum(v, axis=0))
            v = v * step8
        head[:, lane(t)] = jnp.concatenate(pieces, axis=0)
        return carry

    lax.fori_loop(0, tiles, head_tile, 0)
    hspec[...] = jnp.dot(fwd[...], split_rows(head[...]), preferred_element_type=F32) * (1.0 / BLK)
    spec[...] = jnp.dot(fwd[...], split_rows(source[...]), preferred_element_type=F32)

    @pl.when(scans)
    def _():
        rx[p] = parts[tile]

        def earlier(g, s):
            landed(rx.at[pl.ds(0, 8)], out_recv.at[g])
            for n in range(8):
                s = s * through[8 * g + n] + rx[8 * g + n]
            return s

        s = lax.fori_loop(0, group, earlier, jnp.zeros((ORDER, LANES), F32))
        landed(rx.at[pl.ds(0, 7)], out_recv.at[group])

        def own_group(g, s):
            for n in range(8):
                s = s * through[8 * g + n] + rx[8 * g + n]
            return s

        s = lax.fori_loop(group, group + core, own_group, s)

        @pl.when(core == 1)
        def _():
            landed(rx.at[pl.ds(0, 8)], out_recv.at[serves])

        for n in range(8):
            back[n] = s
            if n < 7:
                s = s * through[8 * serves + n] + rx[8 * serves + n]
        for n in range(8):

            @pl.when(8 * serves + n != p)
            def _():
                remote(back.at[n], state.at[tile], back_send.at[n], back_recv.at[0], 8 * serves + n, q).start()

        @pl.when(core == 0)
        def _():
            state[tile] = back[p % 8]

    chans = proj.shape[2]
    for j in range(2):
        cols = slice(j * chans, (j + 1) * chans)
        s_re, s_im = spec[0:BLK, cols], spec[BLK : 2 * BLK, cols]
        h_re, h_im = hspec[0:BLK, :], hspec[BLK : 2 * BLK, :]
        y_re = s_re * h_re - s_im * h_im
        y_im = s_re * h_im + s_im * h_re
        both = jnp.concatenate([y_re, y_im], axis=0)
        intra[j] = jnp.dot(inv[...], split_rows(both), preferred_element_type=F32)
    pass_on(1, 1)

    own_part = jnp.logical_and(scans, core == 0)

    @pl.when(own_part)
    def _():
        landed(state.at[pl.ds(0, 3)], back_recv.at[0])

    @pl.when(jnp.logical_not(own_part))
    def _():
        landed(state, back_recv.at[0])

    def hidden_block(j):
        def hidden_tile(t, carry):
            step8 = lam8[t]
            entering = state[t] * goes0
            if j == 1:
                entering = (lam128[:, lane(t)] * entering + ends_own[:, lane(t)]) * goes1
            v = wide(entering) * reach[t]
            pieces = []
            for k in range(BLK // 8):
                pieces.append(jnp.sum(v, axis=0))
                v = v * step8
            response = intra[j, :, lane(t)] + jnp.concatenate(pieces, axis=0)
            hbuf[q, j * BLK : (j + 1) * BLK, lane(t)] = (query[j, :, lane(t)] * response).astype(BF16)
            return carry

        lax.fori_loop(0, tiles, hidden_tile, 0)

    def piece(b, j):
        return hbuf.at[b, pl.ds(j * BLK, BLK), :]

    def give(idx, b, j, to):
        started(remote(piece(b, j), piece(b, j), hs.at[idx], hr.at[idx], p, to))

    def took(idx, b, j):
        landed(piece(b, j), hr.at[idx])

    hidden_block(0)
    give(0, q, 0, q_right)
    hidden_block(1)
    give(3, q, 1, q_left)
    give(5, q, 1, q_y)
    give(1, q, 1, q_right)
    give(2, q, 0, q_left)
    give(4, q, 0, q_y)
    pass_on(0, 2)
    pass_on(1, 2)
    took(0, q_left, 0)
    give(6, q_left, 0, q_right)
    give(8, q_left, 0, q_y)
    took(5, q_y, 1)
    give(11, q_y, 1, q_left)
    give(10, q_y, 1, q_right)
    took(3, q_right, 1)
    give(7, q_right, 1, q_left)
    pass_on(0, 3)
    took(2, q_right, 0)
    give(9, q_right, 0, q_y)
    pass_on(1, 3)
    took(8, q_yleft, 0)
    give(12, q_yleft, 0, q_right)
    took(11, q_yright, 1)
    give(13, q_yright, 1, q_left)
    pass_on(0, 4)
    pass_on(1, 4)

    for plane in range(2):
        hi = hi_of[plane]
        landed(half(hi, z, 1 - core), wr.at[plane, 6])
        for hop in range(1, 5):
            oz = (z + step * hop + 8) % 8
            landed(wbuf.at[hi, oz] if hop < 4 else half(hi, oz, 1 - core), wr.at[plane, 6 + hop])

    def product(b):
        weights = wbuf[b // 4, pl.ds(2 * (b % 4), 2)].reshape(4 * BLK, acc.shape[1])
        return jnp.dot(hbuf[b], weights, preferred_element_type=F32)

    def project_all(blocks, first):
        for n in range(2):
            cols = slice(n * 256, (n + 1) * 256)
            total = None if first else acc[:, cols]
            for b in blocks:
                weights = wbuf[b // 4, pl.ds(2 * (b % 4), 2), :, cols].reshape(4 * BLK, 256)
                part = jnp.dot(hbuf[b], weights, preferred_element_type=F32)
                total = part if total is None else total + part
            acc[:, cols] = total

    took(1, q_left, 1)
    took(4, q_y, 0)
    project_all((q_y, q, q_right, q_left), True)
    took(6, q_opp, 0)
    took(7, q_opp, 1)
    took(9, q_yright, 0)
    took(10, q_yleft, 1)
    project_all((q_opp, q_yright, q_yleft), False)
    took(12, q_yopp, 0)
    took(13, q_yopp, 1)
    out[...] = (acc[...] + product(q_yopp)).astype(BF16)

    for copy in sends:
        copy.wait_send()

    def handed_out(i, carry):
        @pl.when(scanner(i) != p)
        def _():
            landed(parts.at[i % 4], out_send.at[i])

        return carry

    lax.fori_loop(4 * group, 16, handed_out, 0)

    @pl.when(scans)
    def _():
        for n in range(8):

            @pl.when(8 * serves + n != p)
            def _():
                landed(back.at[n], back_send.at[n])


def shards(fwd, inv, projected, short_filter, residues, decay_rates, doc_blocks, out_weight):
    rows, chans = projected.shape[1:]
    hbm = pl.BlockSpec(memory_space=pltpu.HBM)
    return pl.pallas_call(
        kernel,
        out_shape=pltpu.VMEM((rows, out_weight.shape[1]), BF16),
        in_specs=[hbm] * 8,
        out_specs=pl.BlockSpec(memory_space=pltpu.VMEM),
        scratch_shapes=[
            pltpu.VMEM(projected.shape, BF16),
            pltpu.VMEM(short_filter.shape, F32),
            pltpu.VMEM(residues.shape, F32),
            pltpu.VMEM(decay_rates.shape, F32),
            pltpu.SMEM(doc_blocks.shape, jnp.int32),
            pltpu.VMEM(fwd.shape, BF16),
            pltpu.VMEM(inv.shape, BF16),
            pltpu.VMEM((3, 16, chans), BF16),
            pltpu.VMEM((3, 2, 8 + BLK, chans), F32),
            pltpu.VMEM((2, BLK, chans), F32),
            pltpu.VMEM((BLK, 2 * chans), F32),
            pltpu.VMEM((2 * BLK, 2 * chans), F32),
            pltpu.VMEM((2, BLK, chans), F32),
            pltpu.VMEM((BLK, chans), F32),
            pltpu.VMEM((2 * BLK, chans), F32),
            pltpu.VMEM((4, ORDER, LANES), F32),
            pltpu.VMEM((32, ORDER, LANES), F32),
            pltpu.VMEM((8, ORDER, LANES), F32),
            pltpu.VMEM((4, ORDER, LANES), F32),
            pltpu.VMEM((32, ORDER, LANES), F32),
            pltpu.VMEM((ORDER, chans), F32),
            pltpu.VMEM((ORDER, chans), F32),
            pltpu.VMEM((4, ORDER, 8, LANES), F32),
            pltpu.VMEM((ORDER, chans), F32),
            pltpu.VMEM((4, ORDER, 8, LANES), F32),
            pltpu.VMEM((4, ORDER, 8, LANES), F32),
            pltpu.VMEM((2, 8, 2 * BLK, out_weight.shape[1]), BF16),
            pltpu.VMEM((8, rows, chans), BF16),
            pltpu.VMEM((rows, out_weight.shape[1]), F32),
            pltpu.SemaphoreType.DMA((8,)),
            pltpu.SemaphoreType.DMA((2,)),
            pltpu.SemaphoreType.DMA((16,)),
            pltpu.SemaphoreType.DMA((4,)),
            pltpu.SemaphoreType.DMA((8,)),
            pltpu.SemaphoreType.DMA((1,)),
            pltpu.SemaphoreType.DMA((2, 11)),
            pltpu.SemaphoreType.DMA((2, 11)),
            pltpu.SemaphoreType.DMA((14,)),
            pltpu.SemaphoreType.DMA((14,)),
        ],
        compiler_params=pltpu.CompilerParams(
            collective_id=0, has_side_effects=True, vmem_limit_bytes=60 * 1024 * 1024
        ),
        name="hyena_block",
    )(projected, short_filter, residues, decay_rates, doc_blocks, out_weight, fwd, inv)


def solution(mesh):
    placed = (
        P(None, "ctx", "ch"),
        P(None, None, "ch"),
        P(None, "ch"),
        P(None, "ch"),
        P(),
        P("ctx", "ch"),
    )
    fwd, inv = (jnp.asarray(t) for t in dft_tables())
    return jax.shard_map(
        functools.partial(shards, fwd, inv), mesh=mesh, in_specs=placed, out_specs=P("ctx", "ch"), check_vma=False
    )
```

```python
import functools

import jax
import jax.numpy as jnp
import ml_dtypes
import numpy as np
from jax import lax
from jax.experimental import pallas as pl
from jax.experimental.pallas import tpu as pltpu
from jax.sharding import PartitionSpec as P

ORDER = 16
SHORT = 7
BLK = 128
LANES = 128
MESH = pl.DeviceIdType.MESH
F32, BF16 = jnp.float32, jnp.bfloat16


def dft_tables():
    freq = np.arange(BLK)[:, None] + 0.5
    angles = 2.0 * np.pi * freq * np.arange(BLK)[None, :] / (2 * BLK)
    table = np.concatenate([np.cos(angles), np.sin(angles)], axis=0)

    def split(a):
        high = a.astype(ml_dtypes.bfloat16)
        low = (a - high.astype(np.float64)).astype(ml_dtypes.bfloat16)
        return np.concatenate([high, high, low], axis=1)

    return split(table), split(table.T)


def split_rows(a):
    high = a.astype(BF16)
    low = (a - high.astype(F32)).astype(BF16)
    return jnp.concatenate([high, low, high], axis=0)


def kernel(
    proj_in, sf_in, res_in, dec_in, docs_in, w, fwd_in, inv_in, out,
    proj, sf, res, dec, docs, fwd, inv, halo, ext, query, source, spec, intra, head, hspec,
    parts, rx, back, state, through, ends_own, ends_next, lam8, lam128, first_weight, reach,
    wbuf, hbuf, acc,
    in_sem, halo_sem, out_send, out_recv, back_send, back_recv, ws, wr, hs, hr,
):
    p, q = lax.axis_index("ctx"), lax.axis_index("ch")
    n_ctx = lax.axis_size("ctx")
    core = p % 2
    z = (p // 2) % 8
    y_hi = p // 16
    x, y_lo = q % 4, q // 4

    def ctx_of(hi, zz, cc):
        return hi * 16 + zz * 2 + cc

    q_right = y_lo * 4 + (x + 1) % 4
    q_left = y_lo * 4 + (x + 3) % 4
    q_opp = y_lo * 4 + (x + 2) % 4
    q_y = (1 - y_lo) * 4 + x
    q_yright = (1 - y_lo) * 4 + (x + 1) % 4
    q_yleft = (1 - y_lo) * 4 + (x + 3) % 4
    q_yopp = (1 - y_lo) * 4 + (x + 2) % 4

    def remote(src, dst, send, recv, to_ctx, to_ch):
        return pltpu.make_async_remote_copy(
            src_ref=src, dst_ref=dst, send_sem=send, recv_sem=recv,
            device_id=(to_ctx, to_ch), device_id_type=MESH,
        )

    pairs = ((proj_in, proj), (sf_in, sf), (res_in, res), (dec_in, dec), (docs_in, docs), (fwd_in, fwd), (inv_in, inv))
    loads = [pltpu.make_async_copy(src, dst, in_sem.at[i]) for i, (src, dst) in enumerate(pairs)]
    hi_own = pl.ds(core * 128, 128)
    loads.append(pltpu.make_async_copy(w, wbuf.at[y_hi, z, hi_own, :], in_sem.at[len(pairs)]))
    for load in loads:
        load.start()

    group = p // 8
    scans = z < 4
    serves = 2 * y_hi + core
    tile = z % 4

    def scanner(i):
        return (i // 8) * 16 + (i % 4) * 2 + (i // 4) % 2

    barrier = pltpu.get_barrier_semaphore()

    def greet(to_ctx, to_ch):
        pl.semaphore_signal(barrier, inc=1, device_id=(to_ctx, to_ch), device_id_type=MESH)

    greet((p + n_ctx - 1) % n_ctx, q)
    toward = (z - (1 - 2 * core) + 8) % 8
    for c in range(2):
        greet(ctx_of(y_hi, toward, c), q)
    greet(ctx_of(y_hi, z, 1 - core), q)
    greet(ctx_of(1 - y_hi, z, core), q)
    for to in (q_right, q_left, q_y):
        greet(p, to)

    def greet_scanner(i, carry):
        @pl.when(scanner(i) != p)
        def _():
            greet(scanner(i), q)

        return carry

    lax.fori_loop(4 * group, 4 * group + 4, greet_scanner, 0)

    @pl.when(scans)
    def _():
        def greet_member(n, carry):
            @pl.when(n != p)
            def _():
                greet(n, q)

            return carry

        lax.fori_loop(0, 8 * serves + 8, greet_member, 0)

    own_scan = jnp.where(scans, 1, 0)
    pl.semaphore_wait(barrier, 8 + (16 - 4 * group - own_scan) + own_scan * (7 + core))

    halo_copy = remote(
        proj_in.at[:, pl.ds(240, 16), :], halo, halo_sem.at[0], halo_sem.at[1], (p + 1) % n_ctx, q
    )
    halo_copy.start()

    step = 1 - 2 * core
    z_next = (z + step + 8) % 8
    hi_of = (y_hi, 1 - y_hi)
    sends = []

    def started(copy):
        copy.start()
        sends.append(copy)

    def half(hi, zz, cc):
        return wbuf.at[hi, zz, pl.ds(cc * 128, 128), :]

    def spread(plane, src):
        hi = hi_of[plane]
        dst = half(hi, z, core)
        started(remote(src, dst, ws.at[plane, 1], wr.at[plane, 1 + core], ctx_of(y_hi, (z + 1) % 8, 0), q))
        started(remote(src, dst, ws.at[plane, 2], wr.at[plane, 1 + core], ctx_of(y_hi, (z + 7) % 8, 1), q))
        started(remote(src, dst, ws.at[plane, 6], wr.at[plane, 6], ctx_of(y_hi, z, 1 - core), q))

    def landed(ref, sem):
        pltpu.make_async_copy(ref, ref, sem).wait()

    def pass_on(plane, hop):
        hi = hi_of[plane]
        oz = (z - step * hop + 8) % 8
        whole = wbuf.at[hi, oz]
        mine = half(hi, oz, core)
        if hop == 1:
            landed(half(hi, oz, 0), wr.at[plane, 1])
            landed(half(hi, oz, 1), wr.at[plane, 2])
        elif hop < 4:
            landed(whole, wr.at[plane, 1 + hop])
        else:
            landed(mine, wr.at[plane, 5])
        if hop < 3:
            started(remote(whole, whole, ws.at[plane, 2 + hop], wr.at[plane, 2 + hop], ctx_of(y_hi, z_next, core), q))
        elif hop == 3:
            started(remote(mine, mine, ws.at[plane, 5], wr.at[plane, 5], ctx_of(y_hi, z_next, core), q))
        part = whole if hop < 4 else mine
        started(remote(part, part, ws.at[plane, 6 + hop], wr.at[plane, 6 + hop], ctx_of(y_hi, z, 1 - core), q))

    spread(0, w)
    started(
        remote(w, half(y_hi, z, core), ws.at[1, 0], wr.at[1, 0], ctx_of(1 - y_hi, z, core), q)
    )
    for load in loads:
        load.wait()

    begins0, begins1, at = jnp.float32(0), jnp.float32(0), jnp.int32(0)
    rows = lax.broadcasted_iota(jnp.int32, (32, LANES), 0)
    unbroken = jnp.ones((32, LANES), F32)
    for n in range(docs.shape[0]):
        begins0 = jnp.where(at == 2 * p, 1.0, begins0)
        begins1 = jnp.where(at == 2 * p + 1, 1.0, begins1)
        unbroken = jnp.where(rows == at // 2, 0.0, unbroken)
        at = at + docs[n]
    goes0, goes1 = 1.0 - begins0, 1.0 - begins1

    tiles = proj.shape[2] // LANES
    sub = lax.broadcasted_iota(jnp.int32, (ORDER, 8, LANES), 1).astype(F32)

    def lane(t):
        return pl.ds(pl.multiple_of(t * LANES, LANES), LANES)

    def wide(a):
        return jnp.broadcast_to(a[:, None, :], (ORDER, 8, LANES))

    def wide(a):
        return jnp.broadcast_to(a[:, None, :], (ORDER, 8, LANES))

    def extend(s):
        for j in range(2):
            if j == 1:
                before = proj[s, 112:128, :].astype(F32)[8:16]
                ext[s, j, 0:8, :] = jnp.where(goes1 > 0.5, before, 0.0)
            ext[s, j, 8:136, :] = proj[s, j * BLK : (j + 1) * BLK, :].astype(F32)

    def extend_from_halo(s):
        before = halo[s, :, :].astype(F32)[8:16]
        ext[s, 0, 0:8, :] = jnp.where(goes0 > 0.5, before, 0.0)

    def short(s, j, t, begin, end):
        total = jnp.zeros((end - begin, LANES), F32)
        for tap in range(SHORT):
            total = total + sf[s, tap : tap + 1, lane(t)] * ext[s, j, begin + 8 - tap : end + 8 - tap, lane(t)]
        return total

    def both_lanes(j, t):
        return pl.ds(pl.multiple_of(j * tiles * LANES + t * LANES, LANES), LANES)

    def local_tile(t, carry):
        source[8:BLK, both_lanes(0, t)] = short(1, 0, t, 8, BLK) * short(2, 0, t, 8, BLK)
        source[:, both_lanes(1, t)] = short(1, 1, t, 0, BLK) * short(2, 1, t, 0, BLK)
        d = dec[:, lane(t)]
        step8 = wide(jnp.exp(-8.0 * d))
        lam8[t] = step8
        weight = jnp.exp(-d[:, None, :] * (7.0 - sub))
        for j in range(2):
            total = jnp.zeros((ORDER, 8, LANES), F32)
            for k in range(1 - j, BLK // 8):
                total = total * step8 + source[8 * k : 8 * k + 8, both_lanes(j, t)][None]
            own = jnp.sum(total * weight, axis=1)
            if j == 0:
                ends_own[:, lane(t)] = own
            else:
                ends_next[:, lane(t)] = own
        first_weight[t] = jnp.exp(-d[:, None, :] * (127.0 - sub))
        lam128[:, lane(t)] = jnp.exp(-128.0 * d)
        return carry

    def halo_tile(t, carry):
        first = short(1, 0, t, 0, 8) * short(2, 0, t, 0, 8)
        source[0:8, both_lanes(0, t)] = first
        own = ends_own[:, lane(t)] + jnp.sum(first_weight[t] * first[None], axis=1)
        ends_own[:, lane(t)] = own
        parts[t] = ends_next[:, lane(t)] + lam128[:, lane(t)] * own * goes1
        return carry

    def query_tile(t, carry):
        for j in range(2):
            query[j, :, lane(t)] = short(0, j, t, 0, BLK)
        return carry

    extend(1)
    extend(2)
    lax.fori_loop(0, tiles, local_tile, 0)

    @pl.when(scans)
    def _():
        lam256 = jnp.exp(-256.0 * dec[:, lane(tile)])
        for n in range(32):
            through[n] = lam256 * unbroken[n : n + 1, :]

    halo_copy.wait()
    extend_from_halo(1)
    extend_from_halo(2)
    lax.fori_loop(0, tiles, halo_tile, 0)

    for i in range(16):

        @pl.when(jnp.logical_and(i >= 4 * group, p != scanner(i)))
        def _():
            remote(parts.at[i % 4], rx.at[p], out_send.at[i], out_recv.at[group], scanner(i), q).start()

    seed = half(1 - y_hi, z, core)
    landed(seed, wr.at[1, 0])
    spread(1, seed)
    extend(0)
    extend_from_halo(0)
    lax.fori_loop(0, tiles, query_tile, 0)
    def head_tile(t, carry):
        d = dec[:, lane(t)]
        step8 = lam8[t]
        v = wide(res[:, lane(t)]) * jnp.exp(-d[:, None, :] * sub)
        reach[t] = wide(res[:, lane(t)]) * jnp.exp(-d[:, None, :] * (sub + 1.0))
        pieces = []
        for k in range(BLK // 8):
            pieces.append(jnp.sum(v, axis=0))
            v = v * step8
        head[:, lane(t)] = jnp.concatenate(pieces, axis=0)
        return carry

    lax.fori_loop(0, tiles, head_tile, 0)
    hspec[...] = jnp.dot(fwd[...], split_rows(head[...]), preferred_element_type=F32) * (1.0 / BLK)
    spec[...] = jnp.dot(fwd[...], split_rows(source[...]), preferred_element_type=F32)

    @pl.when(scans)
    def _():
        rx[p] = parts[tile]

        def earlier(g, s):
            landed(rx.at[pl.ds(0, 8)], out_recv.at[g])
            for n in range(8):
                s = s * through[8 * g + n] + rx[8 * g + n]
            return s

        s = lax.fori_loop(0, group, earlier, jnp.zeros((ORDER, LANES), F32))
        landed(rx.at[pl.ds(0, 7)], out_recv.at[group])

        def own_group(g, s):
            for n in range(8):
                s = s * through[8 * g + n] + rx[8 * g + n]
            return s

        s = lax.fori_loop(group, group + core, own_group, s)

        @pl.when(core == 1)
        def _():
            landed(rx.at[pl.ds(0, 8)], out_recv.at[serves])

        for n in range(8):
            back[n] = s
            if n < 7:
                s = s * through[8 * serves + n] + rx[8 * serves + n]
        for n in range(8):

            @pl.when(8 * serves + n != p)
            def _():
                remote(back.at[n], state.at[tile], back_send.at[n], back_recv.at[0], 8 * serves + n, q).start()

        @pl.when(core == 0)
        def _():
            state[tile] = back[p % 8]

    chans = proj.shape[2]
    for j in range(2):
        cols = slice(j * chans, (j + 1) * chans)
        s_re, s_im = spec[0:BLK, cols], spec[BLK : 2 * BLK, cols]
        h_re, h_im = hspec[0:BLK, :], hspec[BLK : 2 * BLK, :]
        y_re = s_re * h_re - s_im * h_im
        y_im = s_re * h_im + s_im * h_re
        both = jnp.concatenate([y_re, y_im], axis=0)
        intra[j] = jnp.dot(inv[...], split_rows(both), preferred_element_type=F32)
    pass_on(0, 1)
    pass_on(1, 1)

    own_part = jnp.logical_and(scans, core == 0)

    @pl.when(own_part)
    def _():
        landed(state.at[pl.ds(0, 3)], back_recv.at[0])

    @pl.when(jnp.logical_not(own_part))
    def _():
        landed(state, back_recv.at[0])

    def hidden_block(j):
        def hidden_tile(t, carry):
            step8 = lam8[t]
            entering = state[t] * goes0
            if j == 1:
                entering = (lam128[:, lane(t)] * entering + ends_own[:, lane(t)]) * goes1
            v = wide(entering) * reach[t]
            pieces = []
            for k in range(BLK // 8):
                pieces.append(jnp.sum(v, axis=0))
                v = v * step8
            response = intra[j, :, lane(t)] + jnp.concatenate(pieces, axis=0)
            hbuf[q, j * BLK : (j + 1) * BLK, lane(t)] = (query[j, :, lane(t)] * response).astype(BF16)
            return carry

        lax.fori_loop(0, tiles, hidden_tile, 0)

    def piece(b, j):
        return hbuf.at[b, pl.ds(j * BLK, BLK), :]

    def give(idx, b, j, to):
        started(remote(piece(b, j), piece(b, j), hs.at[idx], hr.at[idx], p, to))

    def took(idx, b, j):
        landed(piece(b, j), hr.at[idx])

    hidden_block(0)
    give(0, q, 0, q_right)
    hidden_block(1)
    give(3, q, 1, q_left)
    give(5, q, 1, q_y)
    give(1, q, 1, q_right)
    give(2, q, 0, q_left)
    give(4, q, 0, q_y)
    pass_on(0, 2)
    pass_on(1, 2)
    took(0, q_left, 0)
    give(6, q_left, 0, q_right)
    give(8, q_left, 0, q_y)
    took(5, q_y, 1)
    give(11, q_y, 1, q_left)
    give(10, q_y, 1, q_right)
    took(3, q_right, 1)
    give(7, q_right, 1, q_left)
    pass_on(0, 3)
    took(2, q_right, 0)
    give(9, q_right, 0, q_y)
    pass_on(1, 3)
    took(8, q_yleft, 0)
    give(12, q_yleft, 0, q_right)
    took(11, q_yright, 1)
    give(13, q_yright, 1, q_left)
    pass_on(0, 4)
    pass_on(1, 4)

    for plane in range(2):
        hi = hi_of[plane]
        landed(half(hi, z, 1 - core), wr.at[plane, 6])
        for hop in range(1, 5):
            oz = (z + step * hop + 8) % 8
            landed(wbuf.at[hi, oz] if hop < 4 else half(hi, oz, 1 - core), wr.at[plane, 6 + hop])

    def product(b):
        weights = wbuf[b // 4, pl.ds(2 * (b % 4), 2)].reshape(4 * BLK, acc.shape[1])
        return jnp.dot(hbuf[b], weights, preferred_element_type=F32)

    def project_all(blocks, first):
        for n in range(2):
            cols = slice(n * 256, (n + 1) * 256)
            total = None if first else acc[:, cols]
            for b in blocks:
                weights = wbuf[b // 4, pl.ds(2 * (b % 4), 2), :, cols].reshape(4 * BLK, 256)
                part = jnp.dot(hbuf[b], weights, preferred_element_type=F32)
                total = part if total is None else total + part
            acc[:, cols] = total

    took(1, q_left, 1)
    took(4, q_y, 0)
    project_all((q_y, q, q_right, q_left), True)
    took(6, q_opp, 0)
    took(7, q_opp, 1)
    took(9, q_yright, 0)
    took(10, q_yleft, 1)
    project_all((q_opp, q_yright, q_yleft), False)
    took(12, q_yopp, 0)
    took(13, q_yopp, 1)
    out[...] = (acc[...] + product(q_yopp)).astype(BF16)

    for copy in sends:
        copy.wait_send()

    def handed_out(i, carry):
        @pl.when(scanner(i) != p)
        def _():
            landed(parts.at[i % 4], out_send.at[i])

        return carry

    lax.fori_loop(4 * group, 16, handed_out, 0)

    @pl.when(scans)
    def _():
        for n in range(8):

            @pl.when(8 * serves + n != p)
            def _():
                landed(back.at[n], back_send.at[n])


def shards(fwd, inv, projected, short_filter, residues, decay_rates, doc_blocks, out_weight):
    rows, chans = projected.shape[1:]
    hbm = pl.BlockSpec(memory_space=pltpu.HBM)
    return pl.pallas_call(
        kernel,
        out_shape=pltpu.VMEM((rows, out_weight.shape[1]), BF16),
        in_specs=[hbm] * 8,
        out_specs=pl.BlockSpec(memory_space=pltpu.VMEM),
        scratch_shapes=[
            pltpu.VMEM(projected.shape, BF16),
            pltpu.VMEM(short_filter.shape, F32),
            pltpu.VMEM(residues.shape, F32),
            pltpu.VMEM(decay_rates.shape, F32),
            pltpu.SMEM(doc_blocks.shape, jnp.int32),
            pltpu.VMEM(fwd.shape, BF16),
            pltpu.VMEM(inv.shape, BF16),
            pltpu.VMEM((3, 16, chans), BF16),
            pltpu.VMEM((3, 2, 8 + BLK, chans), F32),
            pltpu.VMEM((2, BLK, chans), F32),
            pltpu.VMEM((BLK, 2 * chans), F32),
            pltpu.VMEM((2 * BLK, 2 * chans), F32),
            pltpu.VMEM((2, BLK, chans), F32),
            pltpu.VMEM((BLK, chans), F32),
            pltpu.VMEM((2 * BLK, chans), F32),
            pltpu.VMEM((4, ORDER, LANES), F32),
            pltpu.VMEM((32, ORDER, LANES), F32),
            pltpu.VMEM((8, ORDER, LANES), F32),
            pltpu.VMEM((4, ORDER, LANES), F32),
            pltpu.VMEM((32, ORDER, LANES), F32),
            pltpu.VMEM((ORDER, chans), F32),
            pltpu.VMEM((ORDER, chans), F32),
            pltpu.VMEM((4, ORDER, 8, LANES), F32),
            pltpu.VMEM((ORDER, chans), F32),
            pltpu.VMEM((4, ORDER, 8, LANES), F32),
            pltpu.VMEM((4, ORDER, 8, LANES), F32),
            pltpu.VMEM((2, 8, 2 * BLK, out_weight.shape[1]), BF16),
            pltpu.VMEM((8, rows, chans), BF16),
            pltpu.VMEM((rows, out_weight.shape[1]), F32),
            pltpu.SemaphoreType.DMA((8,)),
            pltpu.SemaphoreType.DMA((2,)),
            pltpu.SemaphoreType.DMA((16,)),
            pltpu.SemaphoreType.DMA((4,)),
            pltpu.SemaphoreType.DMA((8,)),
            pltpu.SemaphoreType.DMA((1,)),
            pltpu.SemaphoreType.DMA((2, 11)),
            pltpu.SemaphoreType.DMA((2, 11)),
            pltpu.SemaphoreType.DMA((14,)),
            pltpu.SemaphoreType.DMA((14,)),
        ],
        compiler_params=pltpu.CompilerParams(
            collective_id=0, has_side_effects=True, vmem_limit_bytes=60 * 1024 * 1024
        ),
        name="hyena_block",
    )(projected, short_filter, residues, decay_rates, doc_blocks, out_weight, fwd, inv)


def solution(mesh):
    placed = (
        P(None, "ctx", "ch"),
        P(None, None, "ch"),
        P(None, "ch"),
        P(None, "ch"),
        P(),
        P("ctx", "ch"),
    )
    fwd, inv = (jnp.asarray(t) for t in dft_tables())
    return jax.shard_map(
        functools.partial(shards, fwd, inv), mesh=mesh, in_specs=placed, out_specs=P("ctx", "ch"), check_vma=False
    )
```

```python
import functools

import jax
import jax.numpy as jnp
import ml_dtypes
import numpy as np
from jax import lax
from jax.experimental import pallas as pl
from jax.experimental.pallas import tpu as pltpu
from jax.sharding import PartitionSpec as P

ORDER = 16
SHORT = 7
BLK = 128
LANES = 128
MESH = pl.DeviceIdType.MESH
F32, BF16 = jnp.float32, jnp.bfloat16


def dft_tables():
    freq = np.arange(BLK)[:, None] + 0.5
    angles = 2.0 * np.pi * freq * np.arange(BLK)[None, :] / (2 * BLK)
    table = np.concatenate([np.cos(angles), np.sin(angles)], axis=0)

    def split(a):
        high = a.astype(ml_dtypes.bfloat16)
        low = (a - high.astype(np.float64)).astype(ml_dtypes.bfloat16)
        return np.concatenate([high, high, low], axis=1)

    return split(table), split(table.T)


def split_rows(a):
    high = a.astype(BF16)
    low = (a - high.astype(F32)).astype(BF16)
    return jnp.concatenate([high, low, high], axis=0)


def kernel(
    proj_in, sf_in, res_in, dec_in, docs_in, w, fwd_in, inv_in, out,
    proj, sf, res, dec, docs, fwd, inv, halo, ext, query, source, spec, intra, head, hspec,
    parts, rx, back, state, through, ends_own, ends_next, lam8, lam128, first_weight, reach,
    wbuf, hbuf, acc,
    in_sem, halo_sem, out_send, out_recv, back_send, back_recv, ws, wr, hs, hr,
):
    p, q = lax.axis_index("ctx"), lax.axis_index("ch")
    n_ctx = lax.axis_size("ctx")
    core = p % 2
    z = (p // 2) % 8
    y_hi = p // 16
    x, y_lo = q % 4, q // 4

    def ctx_of(hi, zz, cc):
        return hi * 16 + zz * 2 + cc

    q_right = y_lo * 4 + (x + 1) % 4
    q_left = y_lo * 4 + (x + 3) % 4
    q_opp = y_lo * 4 + (x + 2) % 4
    q_y = (1 - y_lo) * 4 + x
    q_yright = (1 - y_lo) * 4 + (x + 1) % 4
    q_yleft = (1 - y_lo) * 4 + (x + 3) % 4
    q_yopp = (1 - y_lo) * 4 + (x + 2) % 4

    def remote(src, dst, send, recv, to_ctx, to_ch):
        return pltpu.make_async_remote_copy(
            src_ref=src, dst_ref=dst, send_sem=send, recv_sem=recv,
            device_id=(to_ctx, to_ch), device_id_type=MESH,
        )

    pairs = ((proj_in, proj), (sf_in, sf), (res_in, res), (dec_in, dec), (docs_in, docs), (fwd_in, fwd), (inv_in, inv))
    loads = [pltpu.make_async_copy(src, dst, in_sem.at[i]) for i, (src, dst) in enumerate(pairs)]
    hi_own = pl.ds(core * 128, 128)
    loads.append(pltpu.make_async_copy(w, wbuf.at[y_hi, z, hi_own, :], in_sem.at[len(pairs)]))
    for load in loads:
        load.start()

    group = p // 8
    scans = z < 4
    serves = 2 * y_hi + core
    tile = z % 4

    def scanner(i):
        return (i // 8) * 16 + (i % 4) * 2 + (i // 4) % 2

    barrier = pltpu.get_barrier_semaphore()

    def greet(to_ctx, to_ch):
        pl.semaphore_signal(barrier, inc=1, device_id=(to_ctx, to_ch), device_id_type=MESH)

    greet((p + n_ctx - 1) % n_ctx, q)
    toward = (z - (1 - 2 * core) + 8) % 8
    for c in range(2):
        greet(ctx_of(y_hi, toward, c), q)
    greet(ctx_of(y_hi, z, 1 - core), q)
    greet(ctx_of(1 - y_hi, z, core), q)
    for to in (q_right, q_left, q_y):
        greet(p, to)

    def greet_scanner(i, carry):
        @pl.when(scanner(i) != p)
        def _():
            greet(scanner(i), q)

        return carry

    lax.fori_loop(4 * group, 4 * group + 4, greet_scanner, 0)

    @pl.when(scans)
    def _():
        def greet_member(n, carry):
            @pl.when(n != p)
            def _():
                greet(n, q)

            return carry

        lax.fori_loop(0, 8 * serves + 8, greet_member, 0)

    own_scan = jnp.where(scans, 1, 0)
    pl.semaphore_wait(barrier, 8 + (16 - 4 * group - own_scan) + own_scan * (7 + core))

    halo_copy = remote(
        proj_in.at[:, pl.ds(240, 16), :], halo, halo_sem.at[0], halo_sem.at[1], (p + 1) % n_ctx, q
    )
    halo_copy.start()

    step = 1 - 2 * core
    z_next = (z + step + 8) % 8
    hi_of = (y_hi, 1 - y_hi)
    sends = []

    def started(copy):
        copy.start()
        sends.append(copy)

    def half(hi, zz, cc):
        return wbuf.at[hi, zz, pl.ds(cc * 128, 128), :]

    def spread(plane, src):
        hi = hi_of[plane]
        dst = half(hi, z, core)
        if plane == 0:
            started(remote(src, dst, ws.at[plane, 1], wr.at[plane, 1 + core], ctx_of(y_hi, (z + 1) % 8, 0), q))
            started(remote(src, dst, ws.at[plane, 2], wr.at[plane, 1 + core], ctx_of(y_hi, (z + 7) % 8, 1), q))
        started(remote(src, dst, ws.at[plane, 6], wr.at[plane, 6], ctx_of(y_hi, z, 1 - core), q))

    def landed(ref, sem):
        pltpu.make_async_copy(ref, ref, sem).wait()

    def pass_on(plane, hop):
        hi = hi_of[plane]
        oz = (z - step * hop + 8) % 8
        whole = wbuf.at[hi, oz]
        mine = half(hi, oz, core)
        if plane == 1 and hop == 1:
            landed(whole, wr.at[plane, 1])
        elif hop == 1:
            landed(half(hi, oz, 0), wr.at[plane, 1])
            landed(half(hi, oz, 1), wr.at[plane, 2])
        elif hop < 4:
            landed(whole, wr.at[plane, 1 + hop])
        else:
            landed(mine, wr.at[plane, 5])
        if hop < 3:
            started(remote(whole, whole, ws.at[plane, 2 + hop], wr.at[plane, 2 + hop], ctx_of(y_hi, z_next, core), q))
        elif hop == 3:
            started(remote(mine, mine, ws.at[plane, 5], wr.at[plane, 5], ctx_of(y_hi, z_next, core), q))
        if plane == 0 and hop == 1:
            started(remote(whole, whole, ws.at[1, 1], wr.at[1, 1], ctx_of(1 - y_hi, z, core), q))
        part = whole if hop < 4 else mine
        started(remote(part, part, ws.at[plane, 6 + hop], wr.at[plane, 6 + hop], ctx_of(y_hi, z, 1 - core), q))

    spread(0, w)
    started(
        remote(w, half(y_hi, z, core), ws.at[1, 0], wr.at[1, 0], ctx_of(1 - y_hi, z, core), q)
    )
    for load in loads:
        load.wait()

    begins0, begins1, at = jnp.float32(0), jnp.float32(0), jnp.int32(0)
    rows = lax.broadcasted_iota(jnp.int32, (32, LANES), 0)
    unbroken = jnp.ones((32, LANES), F32)
    for n in range(docs.shape[0]):
        begins0 = jnp.where(at == 2 * p, 1.0, begins0)
        begins1 = jnp.where(at == 2 * p + 1, 1.0, begins1)
        unbroken = jnp.where(rows == at // 2, 0.0, unbroken)
        at = at + docs[n]
    goes0, goes1 = 1.0 - begins0, 1.0 - begins1

    tiles = proj.shape[2] // LANES
    sub = lax.broadcasted_iota(jnp.int32, (ORDER, 8, LANES), 1).astype(F32)

    def lane(t):
        return pl.ds(pl.multiple_of(t * LANES, LANES), LANES)

    def wide(a):
        return jnp.broadcast_to(a[:, None, :], (ORDER, 8, LANES))

    def wide(a):
        return jnp.broadcast_to(a[:, None, :], (ORDER, 8, LANES))

    def extend(s):
        for j in range(2):
            if j == 1:
                before = proj[s, 112:128, :].astype(F32)[8:16]
                ext[s, j, 0:8, :] = jnp.where(goes1 > 0.5, before, 0.0)
            ext[s, j, 8:136, :] = proj[s, j * BLK : (j + 1) * BLK, :].astype(F32)

    def extend_from_halo(s):
        before = halo[s, :, :].astype(F32)[8:16]
        ext[s, 0, 0:8, :] = jnp.where(goes0 > 0.5, before, 0.0)

    def short(s, j, t, begin, end):
        total = jnp.zeros((end - begin, LANES), F32)
        for tap in range(SHORT):
            total = total + sf[s, tap : tap + 1, lane(t)] * ext[s, j, begin + 8 - tap : end + 8 - tap, lane(t)]
        return total

    def both_lanes(j, t):
        return pl.ds(pl.multiple_of(j * tiles * LANES + t * LANES, LANES), LANES)

    def local_tile(t, carry):
        source[8:BLK, both_lanes(0, t)] = short(1, 0, t, 8, BLK) * short(2, 0, t, 8, BLK)
        source[:, both_lanes(1, t)] = short(1, 1, t, 0, BLK) * short(2, 1, t, 0, BLK)
        d = dec[:, lane(t)]
        step8 = wide(jnp.exp(-8.0 * d))
        lam8[t] = step8
        weight = jnp.exp(-d[:, None, :] * (7.0 - sub))
        for j in range(2):
            total = jnp.zeros((ORDER, 8, LANES), F32)
            for k in range(1 - j, BLK // 8):
                total = total * step8 + source[8 * k : 8 * k + 8, both_lanes(j, t)][None]
            own = jnp.sum(total * weight, axis=1)
            if j == 0:
                ends_own[:, lane(t)] = own
            else:
                ends_next[:, lane(t)] = own
        first_weight[t] = jnp.exp(-d[:, None, :] * (127.0 - sub))
        lam128[:, lane(t)] = jnp.exp(-128.0 * d)
        return carry

    def halo_tile(t, carry):
        first = short(1, 0, t, 0, 8) * short(2, 0, t, 0, 8)
        source[0:8, both_lanes(0, t)] = first
        own = ends_own[:, lane(t)] + jnp.sum(first_weight[t] * first[None], axis=1)
        ends_own[:, lane(t)] = own
        parts[t] = ends_next[:, lane(t)] + lam128[:, lane(t)] * own * goes1
        return carry

    def query_tile(t, carry):
        for j in range(2):
            query[j, :, lane(t)] = short(0, j, t, 0, BLK)
        return carry

    extend(1)
    extend(2)
    lax.fori_loop(0, tiles, local_tile, 0)

    @pl.when(scans)
    def _():
        lam256 = jnp.exp(-256.0 * dec[:, lane(tile)])
        for n in range(32):
            through[n] = lam256 * unbroken[n : n + 1, :]

    halo_copy.wait()
    extend_from_halo(1)
    extend_from_halo(2)
    lax.fori_loop(0, tiles, halo_tile, 0)

    for i in range(16):

        @pl.when(jnp.logical_and(i >= 4 * group, p != scanner(i)))
        def _():
            remote(parts.at[i % 4], rx.at[p], out_send.at[i], out_recv.at[group], scanner(i), q).start()

    seed = half(1 - y_hi, z, core)
    pass_on(0, 1)
    landed(seed, wr.at[1, 0])
    spread(1, seed)
    extend(0)
    extend_from_halo(0)
    lax.fori_loop(0, tiles, query_tile, 0)
    def head_tile(t, carry):
        d = dec[:, lane(t)]
        step8 = lam8[t]
        v = wide(res[:, lane(t)]) * jnp.exp(-d[:, None, :] * sub)
        reach[t] = wide(res[:, lane(t)]) * jnp.exp(-d[:, None, :] * (sub + 1.0))
        pieces = []
        for k in range(BLK // 8):
            pieces.append(jnp.sum(v, axis=0))
            v = v * step8
        head[:, lane(t)] = jnp.concatenate(pieces, axis=0)
        return carry

    lax.fori_loop(0, tiles, head_tile, 0)
    hspec[...] = jnp.dot(fwd[...], split_rows(head[...]), preferred_element_type=F32) * (1.0 / BLK)
    spec[...] = jnp.dot(fwd[...], split_rows(source[...]), preferred_element_type=F32)

    @pl.when(scans)
    def _():
        rx[p] = parts[tile]

        def earlier(g, s):
            landed(rx.at[pl.ds(0, 8)], out_recv.at[g])
            for n in range(8):
                s = s * through[8 * g + n] + rx[8 * g + n]
            return s

        s = lax.fori_loop(0, group, earlier, jnp.zeros((ORDER, LANES), F32))
        landed(rx.at[pl.ds(0, 7)], out_recv.at[group])

        def own_group(g, s):
            for n in range(8):
                s = s * through[8 * g + n] + rx[8 * g + n]
            return s

        s = lax.fori_loop(group, group + core, own_group, s)

        @pl.when(core == 1)
        def _():
            landed(rx.at[pl.ds(0, 8)], out_recv.at[serves])

        for n in range(8):
            back[n] = s
            if n < 7:
                s = s * through[8 * serves + n] + rx[8 * serves + n]
        for n in range(8):

            @pl.when(8 * serves + n != p)
            def _():
                remote(back.at[n], state.at[tile], back_send.at[n], back_recv.at[0], 8 * serves + n, q).start()

        @pl.when(core == 0)
        def _():
            state[tile] = back[p % 8]

    chans = proj.shape[2]
    for j in range(2):
        cols = slice(j * chans, (j + 1) * chans)
        s_re, s_im = spec[0:BLK, cols], spec[BLK : 2 * BLK, cols]
        h_re, h_im = hspec[0:BLK, :], hspec[BLK : 2 * BLK, :]
        y_re = s_re * h_re - s_im * h_im
        y_im = s_re * h_im + s_im * h_re
        both = jnp.concatenate([y_re, y_im], axis=0)
        intra[j] = jnp.dot(inv[...], split_rows(both), preferred_element_type=F32)
    pass_on(0, 2)
    pass_on(1, 1)

    own_part = jnp.logical_and(scans, core == 0)

    @pl.when(own_part)
    def _():
        landed(state.at[pl.ds(0, 3)], back_recv.at[0])

    @pl.when(jnp.logical_not(own_part))
    def _():
        landed(state, back_recv.at[0])

    def hidden_block(j):
        def hidden_tile(t, carry):
            step8 = lam8[t]
            entering = state[t] * goes0
            if j == 1:
                entering = (lam128[:, lane(t)] * entering + ends_own[:, lane(t)]) * goes1
            v = wide(entering) * reach[t]
            pieces = []
            for k in range(BLK // 8):
                pieces.append(jnp.sum(v, axis=0))
                v = v * step8
            response = intra[j, :, lane(t)] + jnp.concatenate(pieces, axis=0)
            hbuf[q, j * BLK : (j + 1) * BLK, lane(t)] = (query[j, :, lane(t)] * response).astype(BF16)
            return carry

        lax.fori_loop(0, tiles, hidden_tile, 0)

    spans = {0: (0, BLK), 1: (BLK, BLK), 2: (BLK, 80), 3: (BLK + 80, 48)}

    def piece(b, j):
        return hbuf.at[b, pl.ds(*spans[j]), :]

    def give(idx, b, j, to):
        started(remote(piece(b, j), piece(b, j), hs.at[idx], hr.at[idx], p, to))

    def took(idx, b, j):
        landed(piece(b, j), hr.at[idx])

    hidden_block(0)
    give(0, q, 0, q_right)
    hidden_block(1)
    give(3, q, 1, q_left)
    give(5, q, 1, q_y)
    give(1, q, 1, q_right)
    give(2, q, 0, q_left)
    give(4, q, 0, q_y)
    pass_on(0, 3)
    pass_on(1, 2)
    took(0, q_left, 0)
    give(6, q_left, 0, q_right)
    give(8, q_left, 0, q_y)
    took(5, q_y, 1)
    give(11, q_y, 2, q_left)
    give(10, q_y, 2, q_right)
    took(3, q_right, 1)
    give(7, q_right, 1, q_left)
    give(15, q_right, 3, q_y)
    pass_on(0, 4)
    took(2, q_right, 0)
    give(9, q_right, 0, q_y)
    took(1, q_left, 1)
    give(14, q_left, 3, q_y)
    pass_on(1, 3)
    took(8, q_yleft, 0)
    give(12, q_yleft, 0, q_right)
    took(11, q_yright, 2)
    give(13, q_yright, 2, q_left)
    took(15, q_yright, 3)
    give(16, q_yright, 3, q_left)
    pass_on(1, 4)

    n_early = len(sends) - 12
    for copy in sends[:n_early]:
        copy.wait_send()

    def handed_out(i, carry):
        @pl.when(scanner(i) != p)
        def _():
            landed(parts.at[i % 4], out_send.at[i])

        return carry

    lax.fori_loop(4 * group, 16, handed_out, 0)

    @pl.when(scans)
    def _():
        for n in range(8):

            @pl.when(8 * serves + n != p)
            def _():
                landed(back.at[n], back_send.at[n])

    for plane in range(2):
        hi = hi_of[plane]
        landed(half(hi, z, 1 - core), wr.at[plane, 6])
        for hop in range(1, 5):
            oz = (z + step * hop + 8) % 8
            landed(wbuf.at[hi, oz] if hop < 4 else half(hi, oz, 1 - core), wr.at[plane, 6 + hop])

    def product(b):
        weights = wbuf[b // 4, pl.ds(2 * (b % 4), 2)].reshape(4 * BLK, acc.shape[1])
        return jnp.dot(hbuf[b], weights, preferred_element_type=F32)

    def project_all(blocks, first):
        for n in range(2):
            cols = slice(n * 256, (n + 1) * 256)
            total = None if first else acc[:, cols]
            for b in blocks:
                weights = wbuf[b // 4, pl.ds(2 * (b % 4), 2), :, cols].reshape(4 * BLK, 256)
                part = jnp.dot(hbuf[b], weights, preferred_element_type=F32)
                total = part if total is None else total + part
            acc[:, cols] = total

    took(4, q_y, 0)
    project_all((q_y, q, q_right, q_left), True)
    took(6, q_opp, 0)
    took(7, q_opp, 1)
    took(9, q_yright, 0)
    took(10, q_yleft, 2)
    took(14, q_yleft, 3)
    project_all((q_opp, q_yright, q_yleft), False)
    took(12, q_yopp, 0)
    took(13, q_yopp, 2)
    took(16, q_yopp, 3)
    out[...] = (acc[...] + product(q_yopp)).astype(BF16)

    for copy in sends[n_early:]:
        copy.wait_send()


def shards(fwd, inv, projected, short_filter, residues, decay_rates, doc_blocks, out_weight):
    rows, chans = projected.shape[1:]
    hbm = pl.BlockSpec(memory_space=pltpu.HBM)
    return pl.pallas_call(
        kernel,
        out_shape=pltpu.VMEM((rows, out_weight.shape[1]), BF16),
        in_specs=[hbm] * 8,
        out_specs=pl.BlockSpec(memory_space=pltpu.VMEM),
        scratch_shapes=[
            pltpu.VMEM(projected.shape, BF16),
            pltpu.VMEM(short_filter.shape, F32),
            pltpu.VMEM(residues.shape, F32),
            pltpu.VMEM(decay_rates.shape, F32),
            pltpu.SMEM(doc_blocks.shape, jnp.int32),
            pltpu.VMEM(fwd.shape, BF16),
            pltpu.VMEM(inv.shape, BF16),
            pltpu.VMEM((3, 16, chans), BF16),
            pltpu.VMEM((3, 2, 8 + BLK, chans), F32),
            pltpu.VMEM((2, BLK, chans), F32),
            pltpu.VMEM((BLK, 2 * chans), F32),
            pltpu.VMEM((2 * BLK, 2 * chans), F32),
            pltpu.VMEM((2, BLK, chans), F32),
            pltpu.VMEM((BLK, chans), F32),
            pltpu.VMEM((2 * BLK, chans), F32),
            pltpu.VMEM((4, ORDER, LANES), F32),
            pltpu.VMEM((32, ORDER, LANES), F32),
            pltpu.VMEM((8, ORDER, LANES), F32),
            pltpu.VMEM((4, ORDER, LANES), F32),
            pltpu.VMEM((32, ORDER, LANES), F32),
            pltpu.VMEM((ORDER, chans), F32),
            pltpu.VMEM((ORDER, chans), F32),
            pltpu.VMEM((4, ORDER, 8, LANES), F32),
            pltpu.VMEM((ORDER, chans), F32),
            pltpu.VMEM((4, ORDER, 8, LANES), F32),
            pltpu.VMEM((4, ORDER, 8, LANES), F32),
            pltpu.VMEM((2, 8, 2 * BLK, out_weight.shape[1]), BF16),
            pltpu.VMEM((8, rows, chans), BF16),
            pltpu.VMEM((rows, out_weight.shape[1]), F32),
            pltpu.SemaphoreType.DMA((8,)),
            pltpu.SemaphoreType.DMA((2,)),
            pltpu.SemaphoreType.DMA((16,)),
            pltpu.SemaphoreType.DMA((4,)),
            pltpu.SemaphoreType.DMA((8,)),
            pltpu.SemaphoreType.DMA((1,)),
            pltpu.SemaphoreType.DMA((2, 11)),
            pltpu.SemaphoreType.DMA((2, 11)),
            pltpu.SemaphoreType.DMA((17,)),
            pltpu.SemaphoreType.DMA((17,)),
        ],
        compiler_params=pltpu.CompilerParams(
            collective_id=0, has_side_effects=True, vmem_limit_bytes=60 * 1024 * 1024
        ),
        name="hyena_block",
    )(projected, short_filter, residues, decay_rates, doc_blocks, out_weight, fwd, inv)


def solution(mesh):
    placed = (
        P(None, "ctx", "ch"),
        P(None, None, "ch"),
        P(None, "ch"),
        P(None, "ch"),
        P(),
        P("ctx", "ch"),
    )
    fwd, inv = (jnp.asarray(t) for t in dft_tables())
    return jax.shard_map(
        functools.partial(shards, fwd, inv), mesh=mesh, in_specs=placed, out_specs=P("ctx", "ch"), check_vma=False
    )
```

```python
import functools

import jax
import jax.numpy as jnp
import ml_dtypes
import numpy as np
from jax import lax
from jax.experimental import pallas as pl
from jax.experimental.pallas import tpu as pltpu
from jax.sharding import PartitionSpec as P

ORDER = 16
SHORT = 7
BLK = 128
LANES = 128
MESH = pl.DeviceIdType.MESH
F32, BF16 = jnp.float32, jnp.bfloat16


def dft_tables():
    freq = np.arange(BLK)[:, None] + 0.5
    angles = 2.0 * np.pi * freq * np.arange(BLK)[None, :] / (2 * BLK)
    table = np.concatenate([np.cos(angles), np.sin(angles)], axis=0)

    def split(a):
        high = a.astype(ml_dtypes.bfloat16)
        low = (a - high.astype(np.float64)).astype(ml_dtypes.bfloat16)
        return np.concatenate([high, high, low], axis=1)

    return split(table), split(table.T)


def split_rows(a):
    high = a.astype(BF16)
    low = (a - high.astype(F32)).astype(BF16)
    return jnp.concatenate([high, low, high], axis=0)


def kernel(
    proj_in, sf_in, res_in, dec_in, docs_in, w, fwd_in, inv_in, out,
    proj, sf, res, dec, docs, fwd, inv, halo, ext, query, source, spec, intra, head, hspec,
    parts, rx, back, state, through, ends_own, ends_next, lam8, lam128, first_weight, reach,
    wbuf, hbuf, acc,
    in_sem, halo_sem, out_send, out_recv, back_send, back_recv, ws, wr, hs, hr,
):
    p, q = lax.axis_index("ctx"), lax.axis_index("ch")
    n_ctx = lax.axis_size("ctx")
    core = p % 2
    z = (p // 2) % 8
    y_hi = p // 16
    x, y_lo = q % 4, q // 4

    def ctx_of(hi, zz, cc):
        return hi * 16 + zz * 2 + cc

    q_right = y_lo * 4 + (x + 1) % 4
    q_left = y_lo * 4 + (x + 3) % 4
    q_opp = y_lo * 4 + (x + 2) % 4
    q_y = (1 - y_lo) * 4 + x
    q_yright = (1 - y_lo) * 4 + (x + 1) % 4
    q_yleft = (1 - y_lo) * 4 + (x + 3) % 4
    q_yopp = (1 - y_lo) * 4 + (x + 2) % 4

    def remote(src, dst, send, recv, to_ctx, to_ch):
        return pltpu.make_async_remote_copy(
            src_ref=src, dst_ref=dst, send_sem=send, recv_sem=recv,
            device_id=(to_ctx, to_ch), device_id_type=MESH,
        )

    pairs = ((proj_in, proj), (sf_in, sf), (res_in, res), (dec_in, dec), (docs_in, docs), (fwd_in, fwd), (inv_in, inv))
    loads = [pltpu.make_async_copy(src, dst, in_sem.at[i]) for i, (src, dst) in enumerate(pairs)]
    hi_own = pl.ds(core * 128, 128)
    loads.append(pltpu.make_async_copy(w, wbuf.at[y_hi, z, hi_own, :], in_sem.at[len(pairs)]))
    for load in loads:
        load.start()

    group = p // 8
    scans = z < 4
    serves = 2 * y_hi + core
    tile = z % 4

    def scanner(i):
        return (i // 8) * 16 + (i % 4) * 2 + (i // 4) % 2

    barrier = pltpu.get_barrier_semaphore()

    def greet(to_ctx, to_ch):
        pl.semaphore_signal(barrier, inc=1, device_id=(to_ctx, to_ch), device_id_type=MESH)

    greet((p + n_ctx - 1) % n_ctx, q)
    toward = (z - (1 - 2 * core) + 8) % 8
    for c in range(2):
        greet(ctx_of(y_hi, toward, c), q)
    greet(ctx_of(y_hi, z, 1 - core), q)
    greet(ctx_of(1 - y_hi, z, core), q)
    for to in (q_right, q_left, q_y):
        greet(p, to)

    def greet_scanner(i, carry):
        @pl.when(scanner(i) != p)
        def _():
            greet(scanner(i), q)

        return carry

    lax.fori_loop(4 * group, 4 * group + 4, greet_scanner, 0)

    @pl.when(scans)
    def _():
        def greet_member(n, carry):
            @pl.when(n != p)
            def _():
                greet(n, q)

            return carry

        lax.fori_loop(0, 8 * serves + 8, greet_member, 0)

    own_scan = jnp.where(scans, 1, 0)
    pl.semaphore_wait(barrier, 8 + (16 - 4 * group - own_scan) + own_scan * (7 + core))

    halo_copy = remote(
        proj_in.at[:, pl.ds(240, 16), :], halo, halo_sem.at[0], halo_sem.at[1], (p + 1) % n_ctx, q
    )
    halo_copy.start()

    step = 1 - 2 * core
    z_next = (z + step + 8) % 8
    hi_of = (y_hi, 1 - y_hi)
    sends = []

    def started(copy):
        copy.start()
        sends.append(copy)

    def half(hi, zz, cc):
        return wbuf.at[hi, zz, pl.ds(cc * 128, 128), :]

    def spread(plane, src):
        hi = hi_of[plane]
        dst = half(hi, z, core)
        if plane == 0:
            started(remote(src, dst, ws.at[plane, 1], wr.at[plane, 1 + core], ctx_of(y_hi, (z + 1) % 8, 0), q))
            started(remote(src, dst, ws.at[plane, 2], wr.at[plane, 1 + core], ctx_of(y_hi, (z + 7) % 8, 1), q))
        started(remote(src, dst, ws.at[plane, 6], wr.at[plane, 6], ctx_of(y_hi, z, 1 - core), q))

    def landed(ref, sem):
        pltpu.make_async_copy(ref, ref, sem).wait()

    def pass_on(plane, hop):
        hi = hi_of[plane]
        oz = (z - step * hop + 8) % 8
        whole = wbuf.at[hi, oz]
        mine = half(hi, oz, core)
        if plane == 1 and hop == 1:
            landed(whole, wr.at[plane, 1])
        elif hop == 1:
            landed(half(hi, oz, 0), wr.at[plane, 1])
            landed(half(hi, oz, 1), wr.at[plane, 2])
        elif hop < 4:
            landed(whole, wr.at[plane, 1 + hop])
        else:
            landed(mine, wr.at[plane, 5])
        if hop < 3:
            started(remote(whole, whole, ws.at[plane, 2 + hop], wr.at[plane, 2 + hop], ctx_of(y_hi, z_next, core), q))
        elif hop == 3:
            started(remote(mine, mine, ws.at[plane, 5], wr.at[plane, 5], ctx_of(y_hi, z_next, core), q))
        if plane == 0 and hop == 1:
            started(remote(whole, whole, ws.at[1, 1], wr.at[1, 1], ctx_of(1 - y_hi, z, core), q))
        part = whole if hop < 4 else mine
        started(remote(part, part, ws.at[plane, 6 + hop], wr.at[plane, 6 + hop], ctx_of(y_hi, z, 1 - core), q))

    spread(0, w)
    started(
        remote(w, half(y_hi, z, core), ws.at[1, 0], wr.at[1, 0], ctx_of(1 - y_hi, z, core), q)
    )
    for load in loads:
        load.wait()

    begins0, begins1, at = jnp.float32(0), jnp.float32(0), jnp.int32(0)
    rows = lax.broadcasted_iota(jnp.int32, (32, LANES), 0)
    unbroken = jnp.ones((32, LANES), F32)
    for n in range(docs.shape[0]):
        begins0 = jnp.where(at == 2 * p, 1.0, begins0)
        begins1 = jnp.where(at == 2 * p + 1, 1.0, begins1)
        unbroken = jnp.where(rows == at // 2, 0.0, unbroken)
        at = at + docs[n]
    goes0, goes1 = 1.0 - begins0, 1.0 - begins1

    tiles = proj.shape[2] // LANES
    sub = lax.broadcasted_iota(jnp.int32, (ORDER, 8, LANES), 1).astype(F32)

    def lane(t):
        return pl.ds(pl.multiple_of(t * LANES, LANES), LANES)

    def wide(a):
        return jnp.broadcast_to(a[:, None, :], (ORDER, 8, LANES))

    def wide(a):
        return jnp.broadcast_to(a[:, None, :], (ORDER, 8, LANES))

    def extend(s):
        for j in range(2):
            if j == 1:
                before = proj[s, 112:128, :].astype(F32)[8:16]
                ext[s, j, 0:8, :] = jnp.where(goes1 > 0.5, before, 0.0)
            ext[s, j, 8:136, :] = proj[s, j * BLK : (j + 1) * BLK, :].astype(F32)

    def extend_from_halo(s):
        before = halo[s, :, :].astype(F32)[8:16]
        ext[s, 0, 0:8, :] = jnp.where(goes0 > 0.5, before, 0.0)

    def short(s, j, t, begin, end):
        total = jnp.zeros((end - begin, LANES), F32)
        for tap in range(SHORT):
            total = total + sf[s, tap : tap + 1, lane(t)] * ext[s, j, begin + 8 - tap : end + 8 - tap, lane(t)]
        return total

    def both_lanes(j, t):
        return pl.ds(pl.multiple_of(j * tiles * LANES + t * LANES, LANES), LANES)

    def local_tile(t, carry):
        source[8:BLK, both_lanes(0, t)] = short(1, 0, t, 8, BLK) * short(2, 0, t, 8, BLK)
        source[:, both_lanes(1, t)] = short(1, 1, t, 0, BLK) * short(2, 1, t, 0, BLK)
        d = dec[:, lane(t)]
        step8 = wide(jnp.exp(-8.0 * d))
        lam8[t] = step8
        weight = jnp.exp(-d[:, None, :] * (7.0 - sub))
        for j in range(2):
            total = jnp.zeros((ORDER, 8, LANES), F32)
            for k in range(1 - j, BLK // 8):
                total = total * step8 + source[8 * k : 8 * k + 8, both_lanes(j, t)][None]
            own = jnp.sum(total * weight, axis=1)
            if j == 0:
                ends_own[:, lane(t)] = own
            else:
                ends_next[:, lane(t)] = own
        first_weight[t] = jnp.exp(-d[:, None, :] * (127.0 - sub))
        lam128[:, lane(t)] = jnp.exp(-128.0 * d)
        return carry

    def halo_tile(t, carry):
        first = short(1, 0, t, 0, 8) * short(2, 0, t, 0, 8)
        source[0:8, both_lanes(0, t)] = first
        own = ends_own[:, lane(t)] + jnp.sum(first_weight[t] * first[None], axis=1)
        ends_own[:, lane(t)] = own
        parts[t] = ends_next[:, lane(t)] + lam128[:, lane(t)] * own * goes1
        return carry

    def query_tile(t, carry):
        for j in range(2):
            query[j, :, lane(t)] = short(0, j, t, 0, BLK)
        return carry

    extend(1)
    extend(2)
    lax.fori_loop(0, tiles, local_tile, 0)

    @pl.when(scans)
    def _():
        lam256 = jnp.exp(-256.0 * dec[:, lane(tile)])
        for n in range(32):
            through[n] = lam256 * unbroken[n : n + 1, :]

    halo_copy.wait()
    extend_from_halo(1)
    extend_from_halo(2)
    lax.fori_loop(0, tiles, halo_tile, 0)

    for i in range(16):

        @pl.when(jnp.logical_and(i >= 4 * group, p != scanner(i)))
        def _():
            remote(parts.at[i % 4], rx.at[p], out_send.at[i], out_recv.at[group], scanner(i), q).start()

    seed = half(1 - y_hi, z, core)
    pass_on(0, 1)
    landed(seed, wr.at[1, 0])
    spread(1, seed)
    extend(0)
    extend_from_halo(0)
    lax.fori_loop(0, tiles, query_tile, 0)
    def head_tile(t, carry):
        d = dec[:, lane(t)]
        step8 = lam8[t]
        v = wide(res[:, lane(t)]) * jnp.exp(-d[:, None, :] * sub)
        reach[t] = wide(res[:, lane(t)]) * jnp.exp(-d[:, None, :] * (sub + 1.0))
        pieces = []
        for k in range(BLK // 8):
            pieces.append(jnp.sum(v, axis=0))
            v = v * step8
        head[:, lane(t)] = jnp.concatenate(pieces, axis=0)
        return carry

    lax.fori_loop(0, tiles, head_tile, 0)
    hspec[...] = jnp.dot(fwd[...], split_rows(head[...]), preferred_element_type=F32) * (1.0 / BLK)
    spec[...] = jnp.dot(fwd[...], split_rows(source[...]), preferred_element_type=F32)

    @pl.when(scans)
    def _():
        rx[p] = parts[tile]

        def earlier(g, s):
            landed(rx.at[pl.ds(0, 8)], out_recv.at[g])
            for n in range(8):
                s = s * through[8 * g + n] + rx[8 * g + n]
            return s

        s = lax.fori_loop(0, group, earlier, jnp.zeros((ORDER, LANES), F32))
        landed(rx.at[pl.ds(0, 7)], out_recv.at[group])

        def own_group(g, s):
            for n in range(8):
                s = s * through[8 * g + n] + rx[8 * g + n]
            return s

        s = lax.fori_loop(group, group + core, own_group, s)

        @pl.when(core == 1)
        def _():
            landed(rx.at[pl.ds(0, 8)], out_recv.at[serves])

        for n in range(8):
            back[n] = s
            if n < 7:
                s = s * through[8 * serves + n] + rx[8 * serves + n]
        for n in range(8):

            @pl.when(8 * serves + n != p)
            def _():
                remote(back.at[n], state.at[tile], back_send.at[n], back_recv.at[0], 8 * serves + n, q).start()

        @pl.when(core == 0)
        def _():
            state[tile] = back[p % 8]

    chans = proj.shape[2]
    for j in range(2):
        cols = slice(j * chans, (j + 1) * chans)
        s_re, s_im = spec[0:BLK, cols], spec[BLK : 2 * BLK, cols]
        h_re, h_im = hspec[0:BLK, :], hspec[BLK : 2 * BLK, :]
        y_re = s_re * h_re - s_im * h_im
        y_im = s_re * h_im + s_im * h_re
        both = jnp.concatenate([y_re, y_im], axis=0)
        intra[j] = jnp.dot(inv[...], split_rows(both), preferred_element_type=F32)
    pass_on(0, 2)
    pass_on(1, 1)

    own_part = jnp.logical_and(scans, core == 0)

    @pl.when(own_part)
    def _():
        landed(state.at[pl.ds(0, 3)], back_recv.at[0])

    @pl.when(jnp.logical_not(own_part))
    def _():
        landed(state, back_recv.at[0])

    def hidden_block(j):
        def hidden_tile(t, carry):
            step8 = lam8[t]
            entering = state[t] * goes0
            if j == 1:
                entering = (lam128[:, lane(t)] * entering + ends_own[:, lane(t)]) * goes1
            v = wide(entering) * reach[t]
            pieces = []
            for k in range(BLK // 8):
                pieces.append(jnp.sum(v, axis=0))
                v = v * step8
            response = intra[j, :, lane(t)] + jnp.concatenate(pieces, axis=0)
            hbuf[q, j * BLK : (j + 1) * BLK, lane(t)] = (query[j, :, lane(t)] * response).astype(BF16)
            return carry

        lax.fori_loop(0, tiles, hidden_tile, 0)

    spans = {0: (0, BLK), 1: (BLK, BLK), 2: (BLK, 80), 3: (BLK + 80, 48)}

    def piece(b, j):
        return hbuf.at[b, pl.ds(*spans[j]), :]

    def give(idx, b, j, to):
        started(remote(piece(b, j), piece(b, j), hs.at[idx], hr.at[idx], p, to))

    def took(idx, b, j):
        landed(piece(b, j), hr.at[idx])

    hidden_block(0)
    give(0, q, 0, q_right)
    hidden_block(1)
    give(3, q, 1, q_left)
    give(5, q, 1, q_y)
    give(1, q, 1, q_right)
    give(2, q, 0, q_left)
    give(4, q, 0, q_y)
    pass_on(0, 3)
    pass_on(1, 2)
    took(0, q_left, 0)
    give(6, q_left, 0, q_right)
    give(8, q_left, 0, q_y)
    took(5, q_y, 1)
    give(11, q_y, 2, q_left)
    give(10, q_y, 2, q_right)
    took(3, q_right, 1)
    give(7, q_right, 1, q_left)
    give(15, q_right, 3, q_y)
    pass_on(0, 4)
    pass_on(1, 3)
    took(2, q_right, 0)
    give(9, q_right, 0, q_y)
    took(1, q_left, 1)
    give(14, q_left, 3, q_y)
    took(8, q_yleft, 0)
    give(12, q_yleft, 0, q_right)
    took(11, q_yright, 2)
    give(13, q_yright, 2, q_left)
    took(15, q_yright, 3)
    give(16, q_yright, 3, q_left)
    pass_on(1, 4)

    n_early = len(sends) - 12
    for copy in sends[:n_early]:
        copy.wait_send()

    def handed_out(i, carry):
        @pl.when(scanner(i) != p)
        def _():
            landed(parts.at[i % 4], out_send.at[i])

        return carry

    lax.fori_loop(4 * group, 16, handed_out, 0)

    @pl.when(scans)
    def _():
        for n in range(8):

            @pl.when(8 * serves + n != p)
            def _():
                landed(back.at[n], back_send.at[n])

    for plane in range(2):
        hi = hi_of[plane]
        landed(half(hi, z, 1 - core), wr.at[plane, 6])
        for hop in range(1, 5):
            oz = (z + step * hop + 8) % 8
            landed(wbuf.at[hi, oz] if hop < 4 else half(hi, oz, 1 - core), wr.at[plane, 6 + hop])

    def product(b):
        weights = wbuf[b // 4, pl.ds(2 * (b % 4), 2)].reshape(4 * BLK, acc.shape[1])
        return jnp.dot(hbuf[b], weights, preferred_element_type=F32)

    def project_all(blocks, first):
        for n in range(2):
            cols = slice(n * 256, (n + 1) * 256)
            total = None if first else acc[:, cols]
            for b in blocks:
                weights = wbuf[b // 4, pl.ds(2 * (b % 4), 2), :, cols].reshape(4 * BLK, 256)
                part = jnp.dot(hbuf[b], weights, preferred_element_type=F32)
                total = part if total is None else total + part
            acc[:, cols] = total

    took(4, q_y, 0)
    project_all((q_y, q, q_right, q_left), True)
    took(6, q_opp, 0)
    took(7, q_opp, 1)
    took(9, q_yright, 0)
    took(10, q_yleft, 2)
    took(14, q_yleft, 3)
    project_all((q_opp, q_yright, q_yleft), False)
    took(12, q_yopp, 0)
    took(13, q_yopp, 2)
    took(16, q_yopp, 3)
    out[...] = (acc[...] + product(q_yopp)).astype(BF16)

    for copy in sends[n_early:]:
        copy.wait_send()


def shards(fwd, inv, projected, short_filter, residues, decay_rates, doc_blocks, out_weight):
    rows, chans = projected.shape[1:]
    hbm = pl.BlockSpec(memory_space=pltpu.HBM)
    return pl.pallas_call(
        kernel,
        out_shape=pltpu.VMEM((rows, out_weight.shape[1]), BF16),
        in_specs=[hbm] * 8,
        out_specs=pl.BlockSpec(memory_space=pltpu.VMEM),
        scratch_shapes=[
            pltpu.VMEM(projected.shape, BF16),
            pltpu.VMEM(short_filter.shape, F32),
            pltpu.VMEM(residues.shape, F32),
            pltpu.VMEM(decay_rates.shape, F32),
            pltpu.SMEM(doc_blocks.shape, jnp.int32),
            pltpu.VMEM(fwd.shape, BF16),
            pltpu.VMEM(inv.shape, BF16),
            pltpu.VMEM((3, 16, chans), BF16),
            pltpu.VMEM((3, 2, 8 + BLK, chans), F32),
            pltpu.VMEM((2, BLK, chans), F32),
            pltpu.VMEM((BLK, 2 * chans), F32),
            pltpu.VMEM((2 * BLK, 2 * chans), F32),
            pltpu.VMEM((2, BLK, chans), F32),
            pltpu.VMEM((BLK, chans), F32),
            pltpu.VMEM((2 * BLK, chans), F32),
            pltpu.VMEM((4, ORDER, LANES), F32),
            pltpu.VMEM((32, ORDER, LANES), F32),
            pltpu.VMEM((8, ORDER, LANES), F32),
            pltpu.VMEM((4, ORDER, LANES), F32),
            pltpu.VMEM((32, ORDER, LANES), F32),
            pltpu.VMEM((ORDER, chans), F32),
            pltpu.VMEM((ORDER, chans), F32),
            pltpu.VMEM((4, ORDER, 8, LANES), F32),
            pltpu.VMEM((ORDER, chans), F32),
            pltpu.VMEM((4, ORDER, 8, LANES), F32),
            pltpu.VMEM((4, ORDER, 8, LANES), F32),
            pltpu.VMEM((2, 8, 2 * BLK, out_weight.shape[1]), BF16),
            pltpu.VMEM((8, rows, chans), BF16),
            pltpu.VMEM((rows, out_weight.shape[1]), F32),
            pltpu.SemaphoreType.DMA((8,)),
            pltpu.SemaphoreType.DMA((2,)),
            pltpu.SemaphoreType.DMA((16,)),
            pltpu.SemaphoreType.DMA((4,)),
            pltpu.SemaphoreType.DMA((8,)),
            pltpu.SemaphoreType.DMA((1,)),
            pltpu.SemaphoreType.DMA((2, 11)),
            pltpu.SemaphoreType.DMA((2, 11)),
            pltpu.SemaphoreType.DMA((17,)),
            pltpu.SemaphoreType.DMA((17,)),
        ],
        compiler_params=pltpu.CompilerParams(
            collective_id=0, has_side_effects=True, vmem_limit_bytes=60 * 1024 * 1024
        ),
        name="hyena_block",
    )(projected, short_filter, residues, decay_rates, doc_blocks, out_weight, fwd, inv)


def solution(mesh):
    placed = (
        P(None, "ctx", "ch"),
        P(None, None, "ch"),
        P(None, "ch"),
        P(None, "ch"),
        P(),
        P("ctx", "ch"),
    )
    fwd, inv = (jnp.asarray(t) for t in dft_tables())
    return jax.shard_map(
        functools.partial(shards, fwd, inv), mesh=mesh, in_specs=placed, out_specs=P("ctx", "ch"), check_vma=False
    )
```
